512 devices in a mesh: dec: 128 (over x, z, core), tp: 4 (over y).
Axes of the slice: x: 4, y: 4, z: 16, core: 2. Of those that a mesh axis runs over, the one named last changes fastest.
Arguments:
- hidden_rows: bfloat16 [8, 18432, 7168], P(None, 'dec', 'tp')
- compress_weight: bfloat16 [7168, 576], P('tp')
- latent_gain: float32 [512], replicated, may hold values from 0.25 to 1.75
- segment_page: int32 [18432], replicated, may hold values from 0 to 18431, as said below
- segment_length: int32 [18432], replicated, may hold values from 1 to 8, as said below
- segment_start: int32 [18432], replicated, may hold values from 0 to 4088, as said below
Outputs:
- latent_cache: bfloat16 [8, 18432, 576], P('tp', 'dec')
The draws below stay inside these ranges and needn't reach their ends.
Inputs may be any that keep to these rules, and one draw needn't show every extreme that they name: `segment_page`: a permutation of the pages. Segment s is loaded on dec index s // 144, and its page belongs to the owner segment_page[s] // 144, so every owner receives exactly 144 segments. No dec index loads more than 2 segments for one owner, and some loads exactly 2. `segment_length`: some segment has all 8 rows live. `segment_start`: multiples of 8.
All inputs are finite; a program needn't handle non-finite values.
Results may differ from the reference program's by a relative error of at most 0.0012.
Values may be sent and summed in bfloat16 or wider, within the bound.
A program may use at most 64 MiB of HBM per device.

```python
import math
import jax
import jax.numpy as jnp
from jax import lax

D = 7168
KV_RANK = 512
LAT = 576
SEG = 8
SEGS_DEV = 144
BRANCH = 4096
SEGS = 18432
CAP = 2


def draw_hidden_rows(key, part):
    key = jax.random.fold_in(key, 11)
    key_scale, key_value = jax.random.split(key, 2)
    row_scale = jnp.exp(jax.random.uniform(key_scale, (SEG, SEGS, 1), jnp.float32, math.log(0.3), math.log(3.0)))
    values = jax.random.normal(key_value, (SEG, SEGS, D), jnp.float32)
    values = jnp.clip(values, -6.0, 6.0)
    return (values * row_scale).astype(jnp.bfloat16)


def draw_compress_weight(key, part):
    key = jax.random.fold_in(key, 12)
    key_scale, key_value = jax.random.split(key)
    column_scale = jnp.exp(jax.random.uniform(key_scale, (1, LAT), jnp.float32, math.log(0.3), math.log(3.0)))
    values = jax.random.normal(key_value, (D, LAT), jnp.float32)
    return (values * column_scale / math.sqrt(D)).astype(jnp.bfloat16)


def draw_segment_page(key, part):
    key = jax.random.fold_in(key, 21)
    key_slots, key_shift, key_relabel, key_spread, key_ticket = jax.random.split(key, 5)
    loaders = SEGS // SEGS_DEV
    slot_total = loaders * CAP
    slot_order = jax.random.permutation(key_slots, slot_total)
    slot_ids = jnp.arange(slot_total, dtype=jnp.int32)
    slot_rank = jnp.zeros((slot_total,), jnp.int32).at[slot_order].set(slot_ids)
    forced = slot_order[0] // CAP
    priority = jnp.where(slot_ids // CAP == forced, slot_ids % CAP - CAP, slot_rank)
    chosen = jnp.argsort(priority, stable=True)[:SEGS_DEV]
    offsets = (chosen // CAP).astype(jnp.int32)
    spread = jax.random.permutation(key_spread, jnp.tile(offsets[None, :], (loaders, 1)), axis=1, independent=True)
    shift_in = jax.random.permutation(key_shift, loaders).astype(jnp.int32)
    relabel = jax.random.permutation(key_relabel, loaders).astype(jnp.int32)
    owners = relabel[(shift_in[:, None] + spread) % loaders].reshape(-1)
    ticket = jax.random.permutation(key_ticket, SEGS).astype(jnp.int32)
    sort_key = owners * SEGS + ticket
    sorted_ids = jnp.argsort(sort_key, stable=True)
    return jnp.zeros((SEGS,), jnp.int32).at[sorted_ids].set(jnp.arange(SEGS, dtype=jnp.int32))


def draw_segment_length(key, part):
    key = jax.random.fold_in(key, 22)
    key_limit, key_length, key_pick = jax.random.split(key, 3)
    loaders = SEGS // SEGS_DEV
    row_limit = jax.random.randint(key_limit, (loaders, 1), max(1, SEG // 4), SEG + 1)
    length = jax.random.randint(key_length, (loaders, SEGS_DEV), 1, row_limit + 1).reshape(-1)
    first_pick = jax.random.randint(key_pick, (), 0, SEGS)
    return length.at[first_pick].set(SEG).astype(jnp.int32)


def draw_segment_start(key, part):
    key = jax.random.fold_in(key, 23)
    key_start, key_first, key_second = jax.random.split(key, 3)
    starts = jax.random.randint(key_start, (SEGS,), 0, BRANCH // SEG) * SEG
    first_pick = jax.random.randint(key_first, (), 0, SEGS)
    second_pick = (first_pick + 1 + jax.random.randint(key_second, (), 0, SEGS - 1)) % SEGS
    starts = starts.at[first_pick].set(0).at[second_pick].set(BRANCH - SEG)
    return starts.astype(jnp.int32)


def setup_inputs(seed: int = 0) -> dict:
    keys = jax.random.split(jax.random.key(seed), 7)
    return {
        "hidden_rows": draw_hidden_rows(jax.random.fold_in(keys[6], 71), 0),
        "compress_weight": draw_compress_weight(jax.random.fold_in(keys[6], 71), 0),
        "latent_gain": jnp.clip(1.0 + 0.15 * jax.random.normal(keys[2], (KV_RANK,), jnp.float32), 0.25, 1.75),
        "segment_page": draw_segment_page(jax.random.fold_in(keys[6], 71), 0),
        "segment_length": draw_segment_length(jax.random.fold_in(keys[6], 71), 0),
        "segment_start": draw_segment_start(jax.random.fold_in(keys[6], 71), 0),
    }


def finish_rows(projected, latent_gain, position):
    rank_width = latent_gain.shape[0]
    latent = projected[..., :rank_width]
    rotary = projected[..., rank_width:]
    mean_square = lax.optimization_barrier(jnp.mean(latent * latent, axis=-1, keepdims=True))
    latent = latent / jnp.sqrt(mean_square + 1e-06) * latent_gain
    half_width = rotary.shape[-1] // 2
    exponent = jnp.arange(half_width, dtype=jnp.float32) * (2.0 / rotary.shape[-1])
    frequency = jnp.power(jnp.float32(10000.0), -exponent)
    phase_angle = position[..., None] * frequency
    cosine = jnp.cos(phase_angle)
    sine_part = jnp.sin(phase_angle)
    front_half = rotary[..., :half_width]
    back_half = rotary[..., half_width:]
    return jnp.concatenate([latent, front_half * cosine - back_half * sine_part, back_half * cosine + front_half * sine_part], axis=-1)

def reference(hidden_rows, compress_weight, latent_gain, segment_page, segment_length, segment_start):

    def one_row(row_index):
        row_block = lax.dynamic_index_in_dim(hidden_rows, row_index, 0, keepdims=False)
        projected = jnp.dot(row_block, compress_weight, preferred_element_type=jnp.float32)
        position = (segment_start + row_index).astype(jnp.float32)
        finished = finish_rows(projected, latent_gain, position).astype(jnp.bfloat16)
        live_rows = (row_index < segment_length)[:, None]
        return jnp.where(live_rows, finished, jnp.zeros_like(finished))
    rows_done = lax.map(one_row, jnp.arange(SEG, dtype=jnp.int32))
    return jnp.zeros_like(rows_done).at[:, segment_page].set(rows_done)
```

```python
import functools

import jax
import jax.numpy as jnp
from jax import lax
from jax.experimental import pallas as pl
from jax.experimental.pallas import tpu as pltpu
from jax.sharding import PartitionSpec as P

MESH = pl.DeviceIdType.MESH
TP = 4
NZ = 16
NQ = 8
CAP = 2
SEGS_EACH = 144
RANK = 512
LAT = 576
META = 64
HALF_A = 72
INV_SEGS = 7282


def first_axis_iota(rows, columns):
    return lax.broadcasted_iota(jnp.int32, (rows, columns), 0)


def last_axis_iota(rows, columns):
    return lax.broadcasted_iota(jnp.int32, (rows, columns), 1)


def as_column(row):
    n = row.shape[1]
    same = first_axis_iota(n, n) == last_axis_iota(n, n)
    return jnp.sum(jnp.where(same, row, 0.0), axis=1, keepdims=True)


def as_row(column):
    n = column.shape[0]
    same = first_axis_iota(n, n) == last_axis_iota(n, n)
    return jnp.sum(jnp.where(same, column, 0.0), axis=0, keepdims=True)


def own_entries(ref, own_index):
    offset = own_index * SEGS_EACH
    top = offset // 128
    lane = offset % 128
    first = ref[pl.ds(top, 1), :]
    second = ref[pl.ds(top + 1, 1), :]
    both = jnp.concatenate([first, second], axis=1)
    rolled = pltpu.roll(both, (256 - lane) % 256, axis=1)
    return rolled[:, :SEGS_EACH]


def kernel(
    x_hbm, w_hbm, gain_ref, page_hbm, length_hbm, start_hbm, freq_ref, out_ref,
    x_buf, w_buf, page_buf, length_buf, start_buf,
    part, opp_a, opp_b, from_left, from_right,
    z_send0, z_send1, z_recv0, z_recv1, p_send0, p_send1, p_recv0, p_recv1,
    x_sem, w_sem, i_sem, ys, yr, zs, zr, ps, pr,
):
    dec = lax.axis_index("dec")
    tp = lax.axis_index("tp")
    core = dec % 2
    z = (dec // 2) % NZ
    xx = dec // (2 * NZ)
    plane = xx * 2 + core
    left = (tp + TP - 1) % TP
    right = (tp + 1) % TP
    z_send, z_recv = (z_send0, z_send1), (z_recv0, z_recv1)
    p_send, p_recv = (p_send0, p_send1), (p_recv0, p_recv1)

    def z_device(zz):
        return xx * (2 * NZ) + zz * 2 + core

    def p_device(qq):
        return (qq // 2) * (2 * NZ) + z * 2 + qq % 2

    targets = ((tp + 2) % TP, right, left, tp)
    w_copy = pltpu.make_async_copy(w_hbm, w_buf, w_sem)
    w_copy.start()
    x_copies = [
        pltpu.make_async_copy(x_hbm.at[pl.ds(2 * target, 2)], x_buf.at[i], x_sem.at[i])
        for i, target in enumerate(targets)
    ]
    for copy in x_copies:
        copy.start()
    index_copies = [
        pltpu.make_async_copy(src, dst, i_sem.at[i])
        for i, (src, dst) in enumerate(
            ((page_hbm, page_buf), (length_hbm, length_buf), (start_hbm, start_buf))
        )
    ]
    for copy in index_copies:
        copy.start()

    barrier = pltpu.get_barrier_semaphore()
    for neighbour in (left, right):
        pl.semaphore_signal(barrier, inc=1, device_id=(dec, neighbour), device_id_type=MESH)

    def greet_z(i, carry):
        pl.semaphore_signal(
            barrier, inc=1, device_id=(z_device((z + i) % NZ), tp), device_id_type=MESH
        )
        return carry

    def greet_p(i, carry):
        pl.semaphore_signal(
            barrier, inc=1, device_id=(p_device((plane + i) % NQ), tp), device_id_type=MESH
        )
        return carry

    lax.fori_loop(1, NZ, greet_z, 0)
    lax.fori_loop(1, NQ, greet_p, 0)

    def project(i):
        x_copies[i].wait()
        block = x_buf[i].reshape(2 * SEGS_EACH, x_buf.shape[-1])
        result = jnp.dot(block, w_buf[...], preferred_element_type=jnp.float32)
        part[i] = result.reshape(2, SEGS_EACH, LAT)

    def y_copy(src, dst, rho, kind, target):
        return pltpu.make_async_remote_copy(
            src_ref=src,
            dst_ref=dst,
            send_sem=ys.at[rho, kind],
            recv_sem=yr.at[rho, kind],
            device_id=(dec, target),
            device_id_type=MESH,
        )

    rows_a = pl.ds(0, HALF_A)
    rows_b = pl.ds(HALF_A, SEGS_EACH - HALF_A)
    y_copies = [
        [
            y_copy(part.at[0, rho, rows_a], opp_a.at[rho], rho, 0, right),
            y_copy(part.at[0, rho, rows_b], opp_b.at[rho], rho, 1, left),
            y_copy(part.at[1, rho, rows_b], from_left.at[rho, rows_b], rho, 2, right),
            y_copy(part.at[2, rho, rows_a], from_right.at[rho, rows_a], rho, 3, left),
            y_copy(part.at[1, rho, rows_a], from_left.at[rho, rows_a], rho, 4, right),
            y_copy(part.at[2, rho, rows_b], from_right.at[rho, rows_b], rho, 5, left),
        ]
        for rho in range(2)
    ]

    w_copy.wait()
    project(0)
    pl.semaphore_wait(barrier, 2 + (NZ - 1) + (NQ - 1))
    y_copies[0][0].start()
    y_copies[0][1].start()
    project(1)
    y_copies[0][2].start()
    project(2)
    y_copies[0][3].start()
    y_copies[1][0].start()
    y_copies[1][1].start()
    project(3)

    for copy in index_copies:
        copy.wait()
    page_row = own_entries(page_buf, dec)
    length_row = own_entries(length_buf, dec)
    start_row = own_entries(start_buf, dec)
    owner_row = (page_row * INV_SEGS) >> 20
    place_row = page_row - owner_row * SEGS_EACH
    length_col = as_column(length_row.astype(jnp.float32))
    start_col = as_column(start_row.astype(jnp.float32))
    place_col = as_column(place_row.astype(jnp.float32))
    owner_col = as_column(owner_row.astype(jnp.float32))
    same_owner = owner_col == owner_row.astype(jnp.float32)
    is_earlier = first_axis_iota(SEGS_EACH, SEGS_EACH) < last_axis_iota(SEGS_EACH, SEGS_EACH)
    earlier_row = jnp.sum(
        jnp.where(same_owner, jnp.where(is_earlier, 1.0, 0.0), 0.0), axis=0, keepdims=True
    ).astype(jnp.int32)
    owner_plane = (owner_row >> 5) * 2 + (owner_row & 1)
    owner_z = (owner_row >> 1) & (NZ - 1)
    slot_row = owner_z * (NQ * CAP) + owner_plane * CAP + earlier_row
    slots = NZ * NQ * CAP
    send_table = jnp.where(
        first_axis_iota(slots, SEGS_EACH) == slot_row, 1.0, 0.0
    ).astype(jnp.bfloat16)
    meta = jnp.broadcast_to(place_col + 1.0, (SEGS_EACH, META))

    out_slot = first_axis_iota(slots, slots)
    in_slot = last_axis_iota(slots, slots)
    wanted = ((out_slot >> 1) & (NZ - 1)) * (NQ * CAP) + (out_slot >> 5) * CAP + (out_slot & 1)
    turn_table = jnp.where(wanted == in_slot, 1.0, 0.0).astype(jnp.bfloat16)

    angles = []
    for rho in range(2):
        position = start_col + (2 * tp + rho).astype(jnp.float32)
        phase = position * freq_ref[...]
        angles.append((jnp.cos(phase), jnp.sin(phase)))

    def add_and_pass(rho):
        y_copies[rho][0].wait_recv()
        part[1, rho, rows_a] = part[1, rho, rows_a] + opp_a[rho]
        y_copies[rho][4].start()
        y_copies[rho][1].wait_recv()
        part[2, rho, rows_b] = part[2, rho, rows_b] + opp_b[rho]
        y_copies[rho][5].start()

    add_and_pass(0)
    y_copies[1][2].start()
    y_copies[1][3].start()
    add_and_pass(1)

    def z_copy(rho, other):
        return pltpu.make_async_remote_copy(
            src_ref=z_send[rho].at[other],
            dst_ref=z_recv[rho].at[z],
            send_sem=zs.at[rho, other],
            recv_sem=zr.at[rho, z],
            device_id=(z_device(other), tp),
            device_id_type=MESH,
        )

    def z_arrival(rho, other):
        return pltpu.make_async_remote_copy(
            src_ref=z_send[rho].at[other],
            dst_ref=z_recv[rho].at[other],
            send_sem=zs.at[rho, other],
            recv_sem=zr.at[rho, other],
            device_id=(z_device(other), tp),
            device_id_type=MESH,
        )

    def p_copy(rho, other):
        return pltpu.make_async_remote_copy(
            src_ref=p_send[rho].at[other],
            dst_ref=p_recv[rho].at[plane],
            send_sem=ps.at[rho, other],
            recv_sem=pr.at[rho, plane],
            device_id=(p_device(other), tp),
            device_id_type=MESH,
        )

    def p_arrival(rho, other):
        return pltpu.make_async_remote_copy(
            src_ref=p_send[rho].at[other],
            dst_ref=p_recv[rho].at[other],
            send_sem=ps.at[rho, other],
            recv_sem=pr.at[rho, other],
            device_id=(p_device(other), tp),
            device_id_type=MESH,
        )

    def each(count, me, act):
        def step(i, carry):
            act((me + i) % count)
            return carry

        lax.fori_loop(1, count, step, 0)

    def finish(rho):
        for kind in (2, 3, 4, 5):
            y_copies[rho][kind].wait_recv()
        total = part[3, rho] + from_left[rho] + from_right[rho]
        latent = total[:, :RANK]
        rotary = total[:, RANK:]
        mean_square = jnp.sum(latent * latent, axis=1, keepdims=True) * (1.0 / RANK)
        latent = latent / jnp.sqrt(mean_square + 1e-06) * gain_ref[...]
        half = (LAT - RANK) // 2
        front, back = rotary[:, :half], rotary[:, half:]
        cosine, sine = angles[rho]
        pieces = [latent, front * cosine - back * sine, back * cosine + front * sine]
        row = jnp.concatenate(pieces, axis=1)
        alive = (2 * tp + rho).astype(jnp.float32) < length_col
        row = jnp.where(alive, row, 0.0)
        if rho == 0:
            row = jnp.concatenate([row, meta], axis=1)
        sent = jnp.dot(send_table, row.astype(jnp.bfloat16), preferred_element_type=jnp.float32)
        z_send[rho][...] = sent.astype(jnp.bfloat16).reshape(z_send[rho].shape)
        z_recv[rho][z] = z_send[rho][z]
        each(NZ, z, lambda other: z_copy(rho, other).start())

    def turn(rho):
        each(NZ, z, lambda other: z_arrival(rho, other).wait_recv())
        arrived = z_recv[rho][...].reshape(slots, z_recv[rho].shape[-1])
        turned = jnp.dot(turn_table, arrived, preferred_element_type=jnp.float32)
        p_send[rho][...] = turned.astype(jnp.bfloat16).reshape(p_send[rho].shape)
        p_recv[rho][plane] = p_send[rho][plane]
        each(NQ, plane, lambda other: p_copy(rho, other).start())

    finish(0)
    finish(1)
    turn(0)
    turn(1)
    each(NQ, plane, lambda other: p_arrival(0, other).wait_recv())
    landed = p_recv0[...].reshape(slots, LAT + META)
    place = as_row(landed[:, LAT : LAT + 1].astype(jnp.float32))
    page_ids = (first_axis_iota(SEGS_EACH, slots) + 1).astype(jnp.float32)
    take_table = jnp.where(page_ids == place, 1.0, 0.0).astype(jnp.bfloat16)
    out_ref[0] = jnp.dot(
        take_table, landed[:, :LAT], preferred_element_type=jnp.float32
    ).astype(jnp.bfloat16)
    each(NQ, plane, lambda other: p_arrival(1, other).wait_recv())
    out_ref[1] = jnp.dot(
        take_table, p_recv1[...].reshape(slots, LAT), preferred_element_type=jnp.float32
    ).astype(jnp.bfloat16)

    for rho in range(2):
        for copy in y_copies[rho]:
            copy.wait_send()
        each(NZ, z, lambda other: z_copy(rho, other).wait_send())
        each(NQ, plane, lambda other: p_copy(rho, other).wait_send())


def shards(hidden_rows, compress_weight, latent_gain, segment_page, segment_length, segment_start):
    half = (LAT - RANK) // 2
    exponent = jnp.arange(half, dtype=jnp.float32) * (2.0 / (LAT - RANK))
    frequency = jnp.power(jnp.float32(10000.0), -exponent).reshape(1, half)
    width = hidden_rows.shape[-1]
    any_spec = pl.BlockSpec(memory_space=pltpu.HBM)
    vmem_spec = pl.BlockSpec(memory_space=pltpu.VMEM)
    dma = pltpu.SemaphoreType.DMA
    bf16, f32 = jnp.bfloat16, jnp.float32
    n = SEGS_EACH
    scratch = [
        pltpu.VMEM((TP, 2, n, width), bf16),
        pltpu.VMEM((width, LAT), bf16),
        pltpu.VMEM((n, 128), jnp.int32),
        pltpu.VMEM((n, 128), jnp.int32),
        pltpu.VMEM((n, 128), jnp.int32),
        pltpu.VMEM((TP, 2, n, LAT), f32),
        pltpu.VMEM((2, HALF_A, LAT), f32),
        pltpu.VMEM((2, n - HALF_A, LAT), f32),
        pltpu.VMEM((2, n, LAT), f32),
        pltpu.VMEM((2, n, LAT), f32),
        pltpu.VMEM((NZ, NQ * CAP, LAT + META), bf16),
        pltpu.VMEM((NZ, NQ * CAP, LAT), bf16),
        pltpu.VMEM((NZ, NQ * CAP, LAT + META), bf16),
        pltpu.VMEM((NZ, NQ * CAP, LAT), bf16),
        pltpu.VMEM((NQ, NZ * CAP, LAT + META), bf16),
        pltpu.VMEM((NQ, NZ * CAP, LAT), bf16),
        pltpu.VMEM((NQ, NZ * CAP, LAT + META), bf16),
        pltpu.VMEM((NQ, NZ * CAP, LAT), bf16),
        dma((TP,)),
        dma(()),
        dma((3,)),
        dma((2, 6)),
        dma((2, 6)),
        dma((2, NZ)),
        dma((2, NZ)),
        dma((2, NQ)),
        dma((2, NQ)),
    ]
    return pl.pallas_call(
        kernel,
        out_shape=jax.ShapeDtypeStruct((2, n, LAT), bf16),
        in_specs=[any_spec, any_spec, vmem_spec, any_spec, any_spec, any_spec, vmem_spec],
        out_specs=vmem_spec,
        scratch_shapes=scratch,
        compiler_params=pltpu.CompilerParams(
            collective_id=0, has_side_effects=True, vmem_limit_bytes=50 * 1024 * 1024
        ),
        cost_estimate=pl.CostEstimate(
            flops=2 * 8 * n * width * LAT, bytes_accessed=7_000_000, transcendentals=0
        ),
        name="latent_rows",
    )(
        hidden_rows,
        compress_weight,
        latent_gain.reshape(1, RANK),
        segment_page.reshape(n, 128),
        segment_length.reshape(n, 128),
        segment_start.reshape(n, 128),
        frequency,
    )


def solution(mesh):
    in_specs = (P(None, "dec", "tp"), P("tp", None), P(), P(), P(), P())
    out_specs = P("tp", "dec", None)
    return jax.shard_map(shards, mesh=mesh, in_specs=in_specs, out_specs=out_specs, check_vma=False)
```

```python
import functools

import jax
import jax.numpy as jnp
from jax import lax
from jax.experimental import pallas as pl
from jax.experimental.pallas import tpu as pltpu
from jax.sharding import PartitionSpec as P

MESH = pl.DeviceIdType.MESH
TP = 4
NZ = 16
NQ = 8
CAP = 2
SEGS_EACH = 144
RANK = 512
LAT = 576
META = 64
WIDE = LAT + META
HALF_A = 80
INV_SEGS = 7282


def first_axis_iota(rows, columns):
    return lax.broadcasted_iota(jnp.int32, (rows, columns), 0)


def last_axis_iota(rows, columns):
    return lax.broadcasted_iota(jnp.int32, (rows, columns), 1)


def as_column(row):
    n = row.shape[1]
    same = first_axis_iota(n, n) == last_axis_iota(n, n)
    return jnp.sum(jnp.where(same, row, 0.0), axis=1, keepdims=True)


def as_row(column):
    n = column.shape[0]
    same = first_axis_iota(n, n) == last_axis_iota(n, n)
    return jnp.sum(jnp.where(same, column, 0.0), axis=0, keepdims=True)


def own_entries(ref, own_index):
    offset = own_index * SEGS_EACH
    top = offset // 128
    lane = offset % 128
    first = ref[pl.ds(top, 1), :]
    second = ref[pl.ds(top + 1, 1), :]
    both = jnp.concatenate([first, second], axis=1)
    rolled = pltpu.roll(both, (256 - lane) % 256, axis=1)
    return rolled[:, :SEGS_EACH]


def encode(block):
    latent, rotary = block[:, :RANK], block[:, RANK:]
    codes, pieces = [], []
    for piece in (latent, rotary):
        top = jnp.max(jnp.abs(piece), axis=1, keepdims=True)
        code = jnp.ceil(jnp.log2(jnp.maximum(top, 1e-30)) * 128.0 + 0.01)
        codes.append(code)
        pieces.append(piece * jnp.exp2(14.999 - code * (1.0 / 128.0)))
    lane = last_axis_iota(block.shape[0], META)
    pieces.append(jnp.where(lane < META // 2, codes[0], codes[1]))
    coded = jnp.concatenate(pieces, axis=1)
    return jnp.round(coded).astype(jnp.int32).astype(jnp.int16)


def decode(coded):
    block = coded.astype(jnp.int32).astype(jnp.float32)
    pieces = []
    for columns, place in ((slice(0, RANK), LAT), (slice(RANK, LAT), LAT + META // 2)):
        scale = jnp.exp2(block[:, place : place + 1] * (1.0 / 128.0) - 14.999)
        pieces.append(block[:, columns] * scale)
    return jnp.concatenate(pieces, axis=1)


def kernel(
    x_hbm, w_hbm, gain_ref, page_hbm, length_hbm, start_hbm, freq_ref, out_ref,
    x_buf, w_buf, page_buf, length_buf, start_buf,
    part, to_opposite, to_right, to_left, opposite, from_left, from_right,
    z_send0, z_send1, z_recv0, z_recv1, p_send0, p_send1, p_recv0, p_recv1,
    x_sem, w_sem, i_sem, ys, yr, zs, zr, ps, pr,
):
    dec = lax.axis_index("dec")
    tp = lax.axis_index("tp")
    core = dec % 2
    z = (dec // 2) % NZ
    xx = dec // (2 * NZ)
    plane = xx * 2 + core
    left = (tp + TP - 1) % TP
    right = (tp + 1) % TP
    z_send, z_recv = (z_send0, z_send1), (z_recv0, z_recv1)
    p_send, p_recv = (p_send0, p_send1), (p_recv0, p_recv1)

    def z_device(zz):
        return xx * (2 * NZ) + zz * 2 + core

    def p_device(qq):
        return (qq // 2) * (2 * NZ) + z * 2 + qq % 2

    targets = ((tp + 2) % TP, right, left, tp)
    w_copy = pltpu.make_async_copy(w_hbm, w_buf, w_sem)
    w_copy.start()
    x_copies = [
        pltpu.make_async_copy(x_hbm.at[pl.ds(2 * target, 2)], x_buf.at[i], x_sem.at[i])
        for i, target in enumerate(targets)
    ]
    for copy in x_copies:
        copy.start()
    index_copies = [
        pltpu.make_async_copy(src, dst, i_sem.at[i])
        for i, (src, dst) in enumerate(
            ((page_hbm, page_buf), (length_hbm, length_buf), (start_hbm, start_buf))
        )
    ]
    for copy in index_copies:
        copy.start()

    barrier = pltpu.get_barrier_semaphore()
    for neighbour in (left, right):
        pl.semaphore_signal(barrier, inc=1, device_id=(dec, neighbour), device_id_type=MESH)

    def greet_z(i, carry):
        pl.semaphore_signal(
            barrier, inc=1, device_id=(z_device((z + i) % NZ), tp), device_id_type=MESH
        )
        return carry

    def greet_p(i, carry):
        pl.semaphore_signal(
            barrier, inc=1, device_id=(p_device((plane + i) % NQ), tp), device_id_type=MESH
        )
        return carry

    lax.fori_loop(1, NZ, greet_z, 0)
    lax.fori_loop(1, NQ, greet_p, 0)

    def project(i):
        x_copies[i].wait()
        block = x_buf[i].reshape(2 * SEGS_EACH, x_buf.shape[-1])
        result = lax.dot_general(
            block, w_buf[...], (((1,), (1,)), ((), ())), preferred_element_type=jnp.float32
        )
        part[i] = result.reshape(2, SEGS_EACH, LAT)

    def y_copy(src, dst, rho, kind, target):
        return pltpu.make_async_remote_copy(
            src_ref=src,
            dst_ref=dst,
            send_sem=ys.at[rho, kind],
            recv_sem=yr.at[rho, kind],
            device_id=(dec, target),
            device_id_type=MESH,
        )

    rows_a = pl.ds(0, HALF_A)
    rows_b = pl.ds(HALF_A, SEGS_EACH - HALF_A)
    y_copies = [
        [
            y_copy(to_opposite.at[rho, rows_a], opposite.at[rho, rows_a], rho, 0, right),
            y_copy(to_opposite.at[rho, rows_b], opposite.at[rho, rows_b], rho, 1, left),
            y_copy(to_right.at[rho, rows_b], from_left.at[rho, rows_b], rho, 2, right),
            y_copy(to_left.at[rho, rows_a], from_right.at[rho, rows_a], rho, 3, left),
            y_copy(to_right.at[rho, rows_a], from_left.at[rho, rows_a], rho, 4, right),
            y_copy(to_left.at[rho, rows_b], from_right.at[rho, rows_b], rho, 5, left),
        ]
        for rho in range(2)
    ]

    def send_opposite(rho):
        to_opposite[rho] = encode(part[0, rho])
        y_copies[rho][0].start()
        y_copies[rho][1].start()

    def send_right(rho):
        to_right[rho, rows_b] = encode(part[1, rho, rows_b])
        y_copies[rho][2].start()

    def send_left(rho):
        to_left[rho, rows_a] = encode(part[2, rho, rows_a])
        y_copies[rho][3].start()

    w_copy.wait()
    project(0)
    pl.semaphore_wait(barrier, 2 + (NZ - 1) + (NQ - 1))
    send_opposite(0)
    project(1)
    send_right(0)
    project(2)
    send_left(0)
    send_opposite(1)
    project(3)

    for copy in index_copies:
        copy.wait()
    page_row = own_entries(page_buf, dec)
    length_row = own_entries(length_buf, dec)
    start_row = own_entries(start_buf, dec)
    owner_row = (page_row * INV_SEGS) >> 20
    place_row = page_row - owner_row * SEGS_EACH
    length_col = as_column(length_row.astype(jnp.float32))
    start_col = as_column(start_row.astype(jnp.float32))
    place_col = as_column(place_row.astype(jnp.float32))
    owner_col = as_column(owner_row.astype(jnp.float32))
    same_owner = owner_col == owner_row.astype(jnp.float32)
    is_earlier = first_axis_iota(SEGS_EACH, SEGS_EACH) < last_axis_iota(SEGS_EACH, SEGS_EACH)
    earlier_row = jnp.sum(
        jnp.where(same_owner, jnp.where(is_earlier, 1.0, 0.0), 0.0), axis=0, keepdims=True
    ).astype(jnp.int32)
    owner_plane = (owner_row >> 5) * 2 + (owner_row & 1)
    owner_z = (owner_row >> 1) & (NZ - 1)
    slot_row = owner_z * (NQ * CAP) + owner_plane * CAP + earlier_row
    slots = NZ * NQ * CAP
    send_table = jnp.where(
        first_axis_iota(slots, SEGS_EACH) == slot_row, 1.0, 0.0
    ).astype(jnp.bfloat16)
    meta = jnp.broadcast_to(place_col + 1.0, (SEGS_EACH, META))

    out_slot = first_axis_iota(slots, slots)
    in_slot = last_axis_iota(slots, slots)
    wanted = ((out_slot >> 1) & (NZ - 1)) * (NQ * CAP) + (out_slot >> 5) * CAP + (out_slot & 1)
    turn_table = jnp.where(wanted == in_slot, 1.0, 0.0).astype(jnp.bfloat16)

    angles = []
    for rho in range(2):
        position = start_col + (2 * tp + rho).astype(jnp.float32)
        phase = position * freq_ref[...]
        angles.append((jnp.cos(phase), jnp.sin(phase)))

    def add_and_pass(rho):
        y_copies[rho][0].wait_recv()
        to_right[rho, rows_a] = encode(part[1, rho, rows_a] + decode(opposite[rho, rows_a]))
        y_copies[rho][4].start()
        y_copies[rho][1].wait_recv()
        to_left[rho, rows_b] = encode(part[2, rho, rows_b] + decode(opposite[rho, rows_b]))
        y_copies[rho][5].start()

    add_and_pass(0)
    send_right(1)
    send_left(1)

    def each_z(act):
        def step(i, carry):
            act(i + (i + NZ - z) // NZ)
            return carry

        lax.fori_loop(0, NZ - 1, step, 0)

    def z_copy(rho, other):
        return pltpu.make_async_remote_copy(
            src_ref=z_send[rho].at[other],
            dst_ref=z_recv[rho].at[z],
            send_sem=zs.at[rho, other],
            recv_sem=zr.at[rho, z],
            device_id=(z_device(other), tp),
            device_id_type=MESH,
        )

    def z_arrival(rho, other):
        return pltpu.make_async_remote_copy(
            src_ref=z_send[rho].at[other],
            dst_ref=z_recv[rho].at[other],
            send_sem=zs.at[rho, other],
            recv_sem=zr.at[rho, other],
            device_id=(z_device(other), tp),
            device_id_type=MESH,
        )

    def p_copy(rho, other):
        return pltpu.make_async_remote_copy(
            src_ref=p_send[rho].at[other],
            dst_ref=p_recv[rho].at[plane],
            send_sem=ps.at[rho, other],
            recv_sem=pr.at[rho, plane],
            device_id=(p_device(other), tp),
            device_id_type=MESH,
        )

    def p_arrival(rho, other):
        return pltpu.make_async_remote_copy(
            src_ref=p_send[rho].at[other],
            dst_ref=p_recv[rho].at[other],
            send_sem=ps.at[rho, other],
            recv_sem=pr.at[rho, other],
            device_id=(p_device(other), tp),
            device_id_type=MESH,
        )

    def each(count, me, act):
        def step(i, carry):
            act((me + i) % count)
            return carry

        lax.fori_loop(1, count, step, 0)

    def finish(rho):
        for kind in (2, 3, 4, 5):
            y_copies[rho][kind].wait_recv()
        total = part[3, rho] + decode(from_left[rho]) + decode(from_right[rho])
        latent = total[:, :RANK]
        rotary = total[:, RANK:]
        mean_square = jnp.sum(latent * latent, axis=1, keepdims=True) * (1.0 / RANK)
        latent = latent / jnp.sqrt(mean_square + 1e-06) * gain_ref[...]
        half = (LAT - RANK) // 2
        front, back = rotary[:, :half], rotary[:, half:]
        cosine, sine = angles[rho]
        pieces = [latent, front * cosine - back * sine, back * cosine + front * sine]
        row = jnp.concatenate(pieces, axis=1)
        alive = (2 * tp + rho).astype(jnp.float32) < length_col
        row = jnp.where(alive, row, 0.0)
        if rho == 0:
            row = jnp.concatenate([row, meta], axis=1)
        sent = jnp.dot(send_table, row.astype(jnp.bfloat16), preferred_element_type=jnp.float32)
        z_send[rho][...] = sent.astype(jnp.bfloat16).reshape(z_send[rho].shape)
        z_recv[rho][z] = z_send[rho][z]
        each_z(lambda other: z_copy(rho, other).start())

    def turn(rho):
        each_z(lambda other: z_arrival(rho, other).wait_recv())
        arrived = z_recv[rho][...].reshape(slots, z_recv[rho].shape[-1])
        turned = jnp.dot(turn_table, arrived, preferred_element_type=jnp.float32)
        p_send[rho][...] = turned.astype(jnp.bfloat16).reshape(p_send[rho].shape)
        p_recv[rho][plane] = p_send[rho][plane]
        each(NQ, plane, lambda other: p_copy(rho, other).start())

    finish(0)
    add_and_pass(1)
    finish(1)
    turn(0)
    turn(1)
    each(NQ, plane, lambda other: p_arrival(0, other).wait_recv())
    landed = p_recv0[...].reshape(slots, WIDE)
    place = as_row(landed[:, LAT : LAT + 1].astype(jnp.float32))
    page_ids = (first_axis_iota(SEGS_EACH, slots) + 1).astype(jnp.float32)
    take_table = jnp.where(page_ids == place, 1.0, 0.0).astype(jnp.bfloat16)
    out_ref[0] = jnp.dot(
        take_table, landed[:, :LAT], preferred_element_type=jnp.float32
    ).astype(jnp.bfloat16)
    each(NQ, plane, lambda other: p_arrival(1, other).wait_recv())
    out_ref[1] = jnp.dot(
        take_table, p_recv1[...].reshape(slots, LAT), preferred_element_type=jnp.float32
    ).astype(jnp.bfloat16)

    for rho in range(2):
        for copy in y_copies[rho]:
            copy.wait_send()
        each_z(lambda other: z_copy(rho, other).wait_send())
        each(NQ, plane, lambda other: p_copy(rho, other).wait_send())


def shards(hidden_rows, compress_weight, latent_gain, segment_page, segment_length, segment_start):
    half = (LAT - RANK) // 2
    exponent = jnp.arange(half, dtype=jnp.float32) * (2.0 / (LAT - RANK))
    frequency = jnp.power(jnp.float32(10000.0), -exponent).reshape(1, half)
    width = hidden_rows.shape[-1]
    any_spec = pl.BlockSpec(memory_space=pltpu.HBM)
    vmem_spec = pl.BlockSpec(memory_space=pltpu.VMEM)
    dma = pltpu.SemaphoreType.DMA
    bf16, f32 = jnp.bfloat16, jnp.float32
    n = SEGS_EACH
    scratch = [
        pltpu.VMEM((TP, 2, n, width), bf16),
        pltpu.VMEM((LAT, width), bf16),
        pltpu.VMEM((n, 128), jnp.int32),
        pltpu.VMEM((n, 128), jnp.int32),
        pltpu.VMEM((n, 128), jnp.int32),
        pltpu.VMEM((TP, 2, n, LAT), f32),
        pltpu.VMEM((2, n, WIDE), jnp.int16),
        pltpu.VMEM((2, n, WIDE), jnp.int16),
        pltpu.VMEM((2, n, WIDE), jnp.int16),
        pltpu.VMEM((2, n, WIDE), jnp.int16),
        pltpu.VMEM((2, n, WIDE), jnp.int16),
        pltpu.VMEM((2, n, WIDE), jnp.int16),
        pltpu.VMEM((NZ, NQ * CAP, WIDE), bf16),
        pltpu.VMEM((NZ, NQ * CAP, LAT), bf16),
        pltpu.VMEM((NZ, NQ * CAP, WIDE), bf16),
        pltpu.VMEM((NZ, NQ * CAP, LAT), bf16),
        pltpu.VMEM((NQ, NZ * CAP, WIDE), bf16),
        pltpu.VMEM((NQ, NZ * CAP, LAT), bf16),
        pltpu.VMEM((NQ, NZ * CAP, WIDE), bf16),
        pltpu.VMEM((NQ, NZ * CAP, LAT), bf16),
        dma((TP,)),
        dma(()),
        dma((3,)),
        dma((2, 6)),
        dma((2, 6)),
        dma((2, NZ)),
        dma((2, NZ)),
        dma((2, NQ)),
        dma((2, NQ)),
    ]
    return pl.pallas_call(
        kernel,
        out_shape=jax.ShapeDtypeStruct((2, n, LAT), bf16),
        in_specs=[any_spec, any_spec, vmem_spec, any_spec, any_spec, any_spec, vmem_spec],
        out_specs=vmem_spec,
        scratch_shapes=scratch,
        compiler_params=pltpu.CompilerParams(
            collective_id=0, has_side_effects=True, vmem_limit_bytes=50 * 1024 * 1024
        ),
        cost_estimate=pl.CostEstimate(
            flops=2 * 8 * n * width * LAT, bytes_accessed=7_000_000, transcendentals=0
        ),
        name="latent_rows",
    )(
        hidden_rows,
        compress_weight.T,
        latent_gain.reshape(1, RANK),
        segment_page.reshape(n, 128),
        segment_length.reshape(n, 128),
        segment_start.reshape(n, 128),
        frequency,
    )


def solution(mesh):
    in_specs = (P(None, "dec", "tp"), P("tp", None), P(), P(), P(), P())
    out_specs = P("tp", "dec", None)
    return jax.shard_map(shards, mesh=mesh, in_specs=in_specs, out_specs=out_specs, check_vma=False)
```

```python
import functools

import jax
import jax.numpy as jnp
from jax import lax
from jax.experimental import pallas as pl
from jax.experimental.pallas import tpu as pltpu
from jax.sharding import PartitionSpec as P

MESH = pl.DeviceIdType.MESH
TP = 4
NZ = 16
NQ = 8
CAP = 2
SEGS_EACH = 144
RANK = 512
LAT = 576
META = 64
WIDE = LAT + META
HALVES = 2
INV_SEGS = 7282


def first_axis_iota(rows, columns):
    return lax.broadcasted_iota(jnp.int32, (rows, columns), 0)


def last_axis_iota(rows, columns):
    return lax.broadcasted_iota(jnp.int32, (rows, columns), 1)


def as_column(row):
    n = row.shape[1]
    same = first_axis_iota(n, n) == last_axis_iota(n, n)
    return jnp.sum(jnp.where(same, row, 0.0), axis=1, keepdims=True)


def as_row(column):
    n = column.shape[0]
    same = first_axis_iota(n, n) == last_axis_iota(n, n)
    return jnp.sum(jnp.where(same, column, 0.0), axis=0, keepdims=True)


def own_entries(ref, own_index):
    offset = own_index * SEGS_EACH
    top = offset // 128
    lane = offset % 128
    first = ref[pl.ds(top, 1), :]
    second = ref[pl.ds(top + 1, 1), :]
    both = jnp.concatenate([first, second], axis=1)
    rolled = pltpu.roll(both, (256 - lane) % 256, axis=1)
    return rolled[:, :SEGS_EACH]


def encode(block):
    latent, rotary = block[:, :RANK], block[:, RANK:]
    codes, pieces = [], []
    for piece in (latent, rotary):
        top = jnp.max(jnp.abs(piece), axis=1, keepdims=True)
        code = jnp.ceil(jnp.log2(jnp.maximum(top, 1e-30)) * 128.0 + 0.01)
        codes.append(code)
        pieces.append(piece * jnp.exp2(14.999 - code * (1.0 / 128.0)))
    lane = last_axis_iota(block.shape[0], META)
    pieces.append(jnp.where(lane < META // 2, codes[0], codes[1]))
    coded = jnp.concatenate(pieces, axis=1)
    return jnp.round(coded).astype(jnp.int32).astype(jnp.int16)


def decode(coded):
    block = coded.astype(jnp.int32).astype(jnp.float32)
    pieces = []
    for columns, place in ((slice(0, RANK), LAT), (slice(RANK, LAT), LAT + META // 2)):
        scale = jnp.exp2(block[:, place : place + 1] * (1.0 / 128.0) - 14.999)
        pieces.append(block[:, columns] * scale)
    return jnp.concatenate(pieces, axis=1)


def kernel(
    x_hbm, w_hbm, gain_hbm, page_hbm, length_hbm, start_hbm, freq_hbm, out_ref,
    x_buf, w_buf, gain_buf, page_buf, length_buf, start_buf, freq_buf,
    part, coded, arrived_rows,
    z_send0, z_send1, z_recv0, z_recv1, p_send0, p_send1, p_recv0, p_recv1,
    x_sem, w_sem, i_sem, ys, yr, zs, zr, ps, pr,
):
    dec = lax.axis_index("dec")
    tp = lax.axis_index("tp")
    core = dec % 2
    z = (dec // 2) % NZ
    xx = dec // (2 * NZ)
    plane = xx * 2 + core
    left = (tp + TP - 1) % TP
    right = (tp + 1) % TP
    z_send, z_recv = (z_send0, z_send1), (z_recv0, z_recv1)
    p_send, p_recv = (p_send0, p_send1), (p_recv0, p_recv1)

    def z_device(zz):
        return xx * (2 * NZ) + zz * 2 + core

    def p_device(qq):
        return (qq // 2) * (2 * NZ) + z * 2 + qq % 2

    targets = ((tp + 2) % TP, right, left, tp)
    w_copy = pltpu.make_async_copy(w_hbm, w_buf, w_sem)
    w_copy.start()
    x_copies = [
        pltpu.make_async_copy(x_hbm.at[pl.ds(2 * target, 2)], x_buf.at[i], x_sem.at[i])
        for i, target in enumerate(targets)
    ]
    for copy in x_copies:
        copy.start()
    index_copies = [
        pltpu.make_async_copy(src, dst, i_sem.at[i])
        for i, (src, dst) in enumerate(
            (
                (page_hbm, page_buf),
                (length_hbm, length_buf),
                (start_hbm, start_buf),
                (gain_hbm, gain_buf),
                (freq_hbm, freq_buf),
            )
        )
    ]
    for copy in index_copies:
        copy.start()

    barrier = pltpu.get_barrier_semaphore()
    for neighbour in targets[:3]:
        pl.semaphore_signal(barrier, inc=1, device_id=(dec, neighbour), device_id_type=MESH)

    def greet_z(i, carry):
        pl.semaphore_signal(
            barrier, inc=1, device_id=(z_device((z + i) % NZ), tp), device_id_type=MESH
        )
        return carry

    def greet_p(i, carry):
        pl.semaphore_signal(
            barrier, inc=1, device_id=(p_device((plane + i) % NQ), tp), device_id_type=MESH
        )
        return carry

    lax.fori_loop(1, NZ, greet_z, 0)
    lax.fori_loop(1, NQ, greet_p, 0)

    def project(rho, i):
        result = lax.dot_general(
            x_buf[i, rho], w_buf[...], (((1,), (1,)), ((), ())), preferred_element_type=jnp.float32
        )
        if i == TP - 1:
            part[rho] = result
        else:
            coded[rho, i] = encode(result)

    y_copies = [
        [
            pltpu.make_async_remote_copy(
                src_ref=coded.at[rho, i],
                dst_ref=arrived_rows.at[rho, i],
                send_sem=ys.at[rho, i],
                recv_sem=yr.at[rho, i],
                device_id=(dec, targets[i]),
                device_id_type=MESH,
            )
            for i in range(TP - 1)
        ]
        for rho in range(2)
    ]

    w_copy.wait()
    x_copies[0].wait()
    project(0, 0)
    pl.semaphore_wait(barrier, (TP - 1) + (NZ - 1) + (NQ - 1))
    y_copies[0][0].start()
    for i in range(1, TP):
        x_copies[i].wait()
        project(0, i)
        if i < TP - 1:
            y_copies[0][i].start()

    for copy in index_copies:
        copy.wait()
    page_row = own_entries(page_buf, dec)
    length_row = own_entries(length_buf, dec)
    start_row = own_entries(start_buf, dec)
    owner_row = (page_row * INV_SEGS) >> 20
    place_row = page_row - owner_row * SEGS_EACH
    length_col = as_column(length_row.astype(jnp.float32))
    start_col = as_column(start_row.astype(jnp.float32))
    place_col = as_column(place_row.astype(jnp.float32))
    owner_col = as_column(owner_row.astype(jnp.float32))
    same_owner = owner_col == owner_row.astype(jnp.float32)
    is_earlier = first_axis_iota(SEGS_EACH, SEGS_EACH) < last_axis_iota(SEGS_EACH, SEGS_EACH)
    earlier_row = jnp.sum(
        jnp.where(same_owner, jnp.where(is_earlier, 1.0, 0.0), 0.0), axis=0, keepdims=True
    ).astype(jnp.int32)
    owner_plane = (owner_row >> 5) * 2 + (owner_row & 1)
    owner_z = (owner_row >> 1) & (NZ - 1)
    slot_row = owner_z * (NQ * CAP) + owner_plane * CAP + earlier_row
    slots = NZ * NQ * CAP
    send_table = jnp.where(
        first_axis_iota(slots, SEGS_EACH) == slot_row, 1.0, 0.0
    ).astype(jnp.bfloat16)
    meta = jnp.broadcast_to(place_col + 1.0, (SEGS_EACH, META))

    half_slots = slots // HALVES
    out_slot = first_axis_iota(half_slots, half_slots)
    in_slot = last_axis_iota(half_slots, half_slots)
    z_of_slot = (out_slot // CAP) % (NZ // HALVES)
    plane_of_slot = out_slot // (CAP * NZ // HALVES)
    wanted = z_of_slot * (NQ * CAP) + plane_of_slot * CAP + out_slot % CAP
    turn_table = jnp.where(wanted == in_slot, 1.0, 0.0).astype(jnp.bfloat16)

    angles = []
    for rho in range(2):
        position = start_col + (2 * tp + rho).astype(jnp.float32)
        phase = position * freq_buf[...]
        angles.append((jnp.cos(phase), jnp.sin(phase)))

    for i in range(TP):
        project(1, i)

    def each_z(act):
        def step(i, carry):
            act(i + (i + NZ - z) // NZ)
            return carry

        lax.fori_loop(0, NZ - 1, step, 0)

    def z_copy(rho, other):
        return pltpu.make_async_remote_copy(
            src_ref=z_send[rho].at[other],
            dst_ref=z_recv[rho].at[z],
            send_sem=zs.at[rho, other],
            recv_sem=zr.at[rho, z],
            device_id=(z_device(other), tp),
            device_id_type=MESH,
        )

    def z_arrival(rho, other):
        return pltpu.make_async_remote_copy(
            src_ref=z_send[rho].at[other],
            dst_ref=z_recv[rho].at[other],
            send_sem=zs.at[rho, other],
            recv_sem=zr.at[rho, other],
            device_id=(z_device(other), tp),
            device_id_type=MESH,
        )

    def p_copy(rho, half, other):
        return pltpu.make_async_remote_copy(
            src_ref=p_send[rho].at[half, other],
            dst_ref=p_recv[rho].at[half, plane],
            send_sem=ps.at[rho, half, other],
            recv_sem=pr.at[rho, half, plane],
            device_id=(p_device(other), tp),
            device_id_type=MESH,
        )

    def p_arrival(rho, half, other):
        return pltpu.make_async_remote_copy(
            src_ref=p_send[rho].at[half, other],
            dst_ref=p_recv[rho].at[half, other],
            send_sem=ps.at[rho, half, other],
            recv_sem=pr.at[rho, half, other],
            device_id=(p_device(other), tp),
            device_id_type=MESH,
        )

    def each(count, me, act):
        def step(i, carry):
            act((me + i) % count)
            return carry

        lax.fori_loop(1, count, step, 0)

    def finish(rho):
        total = part[rho]
        for i in range(TP - 1):
            y_copies[rho][i].wait_recv()
            total = total + decode(arrived_rows[rho, i])
        latent = total[:, :RANK]
        rotary = total[:, RANK:]
        mean_square = jnp.sum(latent * latent, axis=1, keepdims=True) * (1.0 / RANK)
        latent = latent / jnp.sqrt(mean_square + 1e-06) * gain_buf[...]
        half = (LAT - RANK) // 2
        front, back = rotary[:, :half], rotary[:, half:]
        cosine, sine = angles[rho]
        pieces = [latent, front * cosine - back * sine, back * cosine + front * sine]
        row = jnp.concatenate(pieces, axis=1)
        alive = (2 * tp + rho).astype(jnp.float32) < length_col
        row = jnp.where(alive, row, 0.0)
        if rho == 0:
            row = jnp.concatenate([row, meta], axis=1)
        sent = jnp.dot(send_table, row.astype(jnp.bfloat16), preferred_element_type=jnp.float32)
        z_send[rho][...] = sent.astype(jnp.bfloat16).reshape(z_send[rho].shape)
        z_recv[rho][z] = z_send[rho][z]
        each_z(lambda other: z_copy(rho, other).start())

    def turn(rho, half):
        def wait_for(i, carry):
            source = half * (NZ // HALVES) + i

            @pl.when(source != z)
            def _():
                z_arrival(rho, source).wait_recv()

            return carry

        lax.fori_loop(0, NZ // HALVES, wait_for, 0)
        wide = z_recv[rho].shape[-1]
        arrived = z_recv[rho][half * (NZ // HALVES) : (half + 1) * (NZ // HALVES)]
        turned = jnp.dot(
            turn_table, arrived.reshape(slots // HALVES, wide), preferred_element_type=jnp.float32
        )
        p_send[rho][half] = turned.astype(jnp.bfloat16).reshape(p_send[rho].shape[1:])
        p_recv[rho][half, plane] = p_send[rho][half, plane]
        each(NQ, plane, lambda other: p_copy(rho, half, other).start())

    def land(rho, take_table):
        for half in range(HALVES):
            each(NQ, plane, lambda other: p_arrival(rho, half, other).wait_recv())
        landed = p_recv[rho][...].reshape(slots, p_recv[rho].shape[-1])
        if rho == 0:
            place = as_row(landed[:, LAT : LAT + 1].astype(jnp.float32))
            page_ids = (first_axis_iota(SEGS_EACH, slots) + 1).astype(jnp.float32)
            take_table = jnp.where(page_ids == place, 1.0, 0.0).astype(jnp.bfloat16)
        out_ref[rho] = jnp.dot(
            take_table, landed[:, :LAT], preferred_element_type=jnp.float32
        ).astype(jnp.bfloat16)
        return take_table

    finish(0)
    for i in range(TP - 1):
        y_copies[1][i].start()
    finish(1)
    turn(0, 0)
    turn(0, 1)
    turn(1, 0)
    take_table = land(0, None)
    turn(1, 1)
    land(1, take_table)

    for rho in range(2):
        for copy in y_copies[rho]:
            copy.wait_send()
        each_z(lambda other: z_copy(rho, other).wait_send())
        for half in range(HALVES):
            each(NQ, plane, lambda other: p_copy(rho, half, other).wait_send())


def shards(hidden_rows, compress_weight, latent_gain, segment_page, segment_length, segment_start):
    half = (LAT - RANK) // 2
    exponent = jnp.arange(half, dtype=jnp.float32) * (2.0 / (LAT - RANK))
    frequency = jnp.power(jnp.float32(10000.0), -exponent).reshape(1, half)
    width = hidden_rows.shape[-1]
    any_spec = pl.BlockSpec(memory_space=pltpu.HBM)
    vmem_spec = pl.BlockSpec(memory_space=pltpu.VMEM)
    dma = pltpu.SemaphoreType.DMA
    bf16, f32 = jnp.bfloat16, jnp.float32
    n = SEGS_EACH
    slot_rows = NZ // HALVES * CAP
    scratch = [
        pltpu.VMEM((TP, 2, n, width), bf16),
        pltpu.VMEM((LAT, width), bf16),
        pltpu.VMEM((1, RANK), f32),
        pltpu.VMEM((n, 128), jnp.int32),
        pltpu.VMEM((n, 128), jnp.int32),
        pltpu.VMEM((n, 128), jnp.int32),
        pltpu.VMEM((1, half), f32),
        pltpu.VMEM((2, n, LAT), f32),
        pltpu.VMEM((2, TP - 1, n, WIDE), jnp.int16),
        pltpu.VMEM((2, TP - 1, n, WIDE), jnp.int16),
        pltpu.VMEM((NZ, NQ * CAP, WIDE), bf16),
        pltpu.VMEM((NZ, NQ * CAP, LAT), bf16),
        pltpu.VMEM((NZ, NQ * CAP, WIDE), bf16),
        pltpu.VMEM((NZ, NQ * CAP, LAT), bf16),
        pltpu.VMEM((HALVES, NQ, slot_rows, WIDE), bf16),
        pltpu.VMEM((HALVES, NQ, slot_rows, LAT), bf16),
        pltpu.VMEM((HALVES, NQ, slot_rows, WIDE), bf16),
        pltpu.VMEM((HALVES, NQ, slot_rows, LAT), bf16),
        dma((TP,)),
        dma(()),
        dma((5,)),
        dma((2, TP - 1)),
        dma((2, TP - 1)),
        dma((2, NZ)),
        dma((2, NZ)),
        dma((2, HALVES, NQ)),
        dma((2, HALVES, NQ)),
    ]
    return pl.pallas_call(
        kernel,
        out_shape=jax.ShapeDtypeStruct((2, n, LAT), bf16),
        in_specs=[any_spec] * 7,
        out_specs=vmem_spec,
        scratch_shapes=scratch,
        compiler_params=pltpu.CompilerParams(
            collective_id=0, has_side_effects=True, vmem_limit_bytes=60 * 1024 * 1024
        ),
        cost_estimate=pl.CostEstimate(
            flops=2 * 8 * n * width * LAT, bytes_accessed=7_000_000, transcendentals=0
        ),
        name="latent_rows",
    )(
        hidden_rows,
        compress_weight.T,
        latent_gain.reshape(1, RANK),
        segment_page.reshape(n, 128),
        segment_length.reshape(n, 128),
        segment_start.reshape(n, 128),
        frequency,
    )


def solution(mesh):
    in_specs = (P(None, "dec", "tp"), P("tp", None), P(), P(), P(), P())
    out_specs = P("tp", "dec", None)
    return jax.shard_map(shards, mesh=mesh, in_specs=in_specs, out_specs=out_specs, check_vma=False)
```

```python
import functools

import jax
import jax.numpy as jnp
import numpy as np
from jax import lax
from jax.experimental import pallas as pl
from jax.experimental.pallas import tpu as pltpu
from jax.sharding import PartitionSpec as P

MESH = pl.DeviceIdType.MESH
TP = 4
NZ = 16
NQ = 8
CAP = 2
SEGS_EACH = 144
RANK = 512
LAT = 576
META = 64
WIDE = LAT + META
HALF_A = 80
INV_SEGS = 7282


def first_axis_iota(rows, columns):
    return lax.broadcasted_iota(jnp.int32, (rows, columns), 0)


def last_axis_iota(rows, columns):
    return lax.broadcasted_iota(jnp.int32, (rows, columns), 1)


def as_column(row):
    n = row.shape[1]
    same = first_axis_iota(n, n) == last_axis_iota(n, n)
    return jnp.sum(jnp.where(same, row, 0.0), axis=1, keepdims=True)


def as_row(column):
    n = column.shape[0]
    same = first_axis_iota(n, n) == last_axis_iota(n, n)
    return jnp.sum(jnp.where(same, column, 0.0), axis=0, keepdims=True)


def own_entries(ref, own_index):
    offset = own_index * SEGS_EACH
    top = offset // 128
    lane = offset % 128
    first = ref[pl.ds(top, 1), :]
    second = ref[pl.ds(top + 1, 1), :]
    both = jnp.concatenate([first, second], axis=1)
    rolled = pltpu.roll(both, (256 - lane) % 256, axis=1)
    return rolled[:, :SEGS_EACH]


def encode(block):
    latent, rotary = block[:, :RANK], block[:, RANK:]
    codes, pieces = [], []
    for piece in (latent, rotary):
        top = jnp.max(jnp.abs(piece), axis=1, keepdims=True)
        code = jnp.ceil(jnp.log2(jnp.maximum(top, 1e-30)) * 128.0 + 0.01)
        codes.append(code)
        pieces.append(piece * jnp.exp2(14.999 - code * (1.0 / 128.0)))
    lane = last_axis_iota(block.shape[0], META)
    pieces.append(jnp.where(lane < META // 2, codes[0], codes[1]))
    coded = jnp.concatenate(pieces, axis=1)
    return jnp.round(coded).astype(jnp.int32).astype(jnp.int16)


def decode(coded):
    block = coded.astype(jnp.int32).astype(jnp.float32)
    pieces = []
    for columns, place in ((slice(0, RANK), LAT), (slice(RANK, LAT), LAT + META // 2)):
        scale = jnp.exp2(block[:, place : place + 1] * (1.0 / 128.0) - 14.999)
        pieces.append(block[:, columns] * scale)
    return jnp.concatenate(pieces, axis=1)


def kernel(
    x_hbm, w_hbm, gain_hbm, page_hbm, length_hbm, start_hbm, freq_hbm, out_ref,
    x_buf, w_buf, gain_buf, page_buf, length_buf, start_buf, freq_buf,
    part, to_opposite, to_right, to_left, opposite, from_left, from_right,
    z_send0, z_send1, z_recv0, z_recv1, p_send0, p_send1, p_recv0, p_recv1,
    x_sem, w_sem, i_sem, ys, yr, zs, zr, ps, pr,
):
    dec = lax.axis_index("dec")
    tp = lax.axis_index("tp")
    core = dec % 2
    z = (dec // 2) % NZ
    xx = dec // (2 * NZ)
    plane = xx * 2 + core
    left = (tp + TP - 1) % TP
    right = (tp + 1) % TP
    z_send, z_recv = (z_send0, z_send1), (z_recv0, z_recv1)
    p_send, p_recv = (p_send0, p_send1), (p_recv0, p_recv1)

    def z_device(zz):
        return xx * (2 * NZ) + zz * 2 + core

    def p_device(qq):
        return (qq // 2) * (2 * NZ) + z * 2 + qq % 2

    targets = ((tp + 2) % TP, right, left, tp)
    w_copy = pltpu.make_async_copy(w_hbm, w_buf, w_sem)
    w_copy.start()
    x_copies = [
        pltpu.make_async_copy(x_hbm.at[pl.ds(2 * target, 2)], x_buf.at[i], x_sem.at[i])
        for i, target in enumerate(targets)
    ]
    for copy in x_copies:
        copy.start()
    index_copies = [
        pltpu.make_async_copy(src, dst, i_sem.at[i])
        for i, (src, dst) in enumerate(
            (
                (page_hbm, page_buf),
                (length_hbm, length_buf),
                (start_hbm, start_buf),
                (gain_hbm, gain_buf),
                (freq_hbm, freq_buf),
            )
        )
    ]
    for copy in index_copies:
        copy.start()

    barrier = pltpu.get_barrier_semaphore()
    for neighbour in (left, right):
        pl.semaphore_signal(barrier, inc=1, device_id=(dec, neighbour), device_id_type=MESH)

    def greet_z(i, carry):
        pl.semaphore_signal(
            barrier, inc=1, device_id=(z_device((z + i) % NZ), tp), device_id_type=MESH
        )
        return carry

    def greet_p(i, carry):
        pl.semaphore_signal(
            barrier, inc=1, device_id=(p_device((plane + i) % NQ), tp), device_id_type=MESH
        )
        return carry

    lax.fori_loop(1, NZ, greet_z, 0)
    lax.fori_loop(1, NQ, greet_p, 0)

    rows_a = pl.ds(0, HALF_A)
    rows_b = pl.ds(HALF_A, SEGS_EACH - HALF_A)

    def project(rho, i):
        return lax.dot_general(
            x_buf[i, rho], w_buf[...], (((1,), (1,)), ((), ())), preferred_element_type=jnp.float32
        )

    def y_copy(src, dst, rho, kind, target):
        return pltpu.make_async_remote_copy(
            src_ref=src,
            dst_ref=dst,
            send_sem=ys.at[rho, kind],
            recv_sem=yr.at[rho, kind],
            device_id=(dec, target),
            device_id_type=MESH,
        )

    y_copies = [
        [
            y_copy(to_opposite.at[rho, rows_a], opposite.at[rho, rows_a], rho, 0, right),
            y_copy(to_opposite.at[rho, rows_b], opposite.at[rho, rows_b], rho, 1, left),
            y_copy(to_right.at[rho, rows_b], from_left.at[rho, rows_b], rho, 2, right),
            y_copy(to_left.at[rho, rows_a], from_right.at[rho, rows_a], rho, 3, left),
            y_copy(to_right.at[rho, rows_a], from_left.at[rho, rows_a], rho, 4, right),
            y_copy(to_left.at[rho, rows_b], from_right.at[rho, rows_b], rho, 5, left),
        ]
        for rho in range(2)
    ]

    def project_right(rho):
        result = project(rho, 1)
        to_right[rho, rows_b] = encode(result[HALF_A:])
        part[rho, 1, rows_a] = result[:HALF_A]

    def project_left(rho):
        result = project(rho, 2)
        to_left[rho, rows_a] = encode(result[:HALF_A])
        part[rho, 2, rows_b] = result[HALF_A:]

    def start(rho, *kinds):
        for kind in kinds:
            y_copies[rho][kind].start()

    def add_and_pass(rho):
        y_copies[rho][0].wait_recv()
        to_right[rho, rows_a] = encode(part[rho, 1, rows_a] + decode(opposite[rho, rows_a]))
        start(rho, 4)
        y_copies[rho][1].wait_recv()
        to_left[rho, rows_b] = encode(part[rho, 2, rows_b] + decode(opposite[rho, rows_b]))
        start(rho, 5)

    w_copy.wait()
    x_copies[0].wait()
    to_opposite[0] = encode(project(0, 0))
    pl.semaphore_wait(barrier, 2 + (NZ - 1) + (NQ - 1))
    start(0, 0, 1)
    x_copies[1].wait()
    project_right(0)
    start(0, 2)
    x_copies[2].wait()
    project_left(0)
    start(0, 3)
    x_copies[3].wait()
    part[0, 0] = project(0, 3)

    for copy in index_copies:
        copy.wait()
    page_row = own_entries(page_buf, dec)
    length_row = own_entries(length_buf, dec)
    start_row = own_entries(start_buf, dec)
    owner_row = (page_row * INV_SEGS) >> 20
    place_row = page_row - owner_row * SEGS_EACH
    length_col = as_column(length_row.astype(jnp.float32))
    start_col = as_column(start_row.astype(jnp.float32))
    place_col = as_column(place_row.astype(jnp.float32))
    owner_col = as_column(owner_row.astype(jnp.float32))
    same_owner = owner_col == owner_row.astype(jnp.float32)
    is_earlier = first_axis_iota(SEGS_EACH, SEGS_EACH) < last_axis_iota(SEGS_EACH, SEGS_EACH)
    earlier_row = jnp.sum(
        jnp.where(same_owner, jnp.where(is_earlier, 1.0, 0.0), 0.0), axis=0, keepdims=True
    ).astype(jnp.int32)
    owner_plane = (owner_row >> 5) * 2 + (owner_row & 1)
    owner_z = (owner_row >> 1) & (NZ - 1)
    slots = NZ * NQ * CAP
    slot_rows = (
        owner_z * (NQ * CAP) + owner_plane * CAP + earlier_row,
        owner_plane * (NZ * CAP) + owner_z * CAP + earlier_row,
    )
    send_tables = [
        jnp.where(first_axis_iota(slots, SEGS_EACH) == row, 1.0, 0.0).astype(jnp.bfloat16)
        for row in slot_rows
    ]
    meta = jnp.broadcast_to(place_col + 1.0, (SEGS_EACH, META))

    by_plane = first_axis_iota(slots, slots)
    by_z = last_axis_iota(slots, slots)
    wanted = ((by_plane // CAP) % NZ) * (NQ * CAP) + by_plane // (CAP * NZ) * CAP + by_plane % CAP
    to_plane_order = jnp.where(wanted == by_z, 1.0, 0.0).astype(jnp.bfloat16)
    by_z, by_plane = first_axis_iota(slots, slots), last_axis_iota(slots, slots)
    wanted = ((by_z // CAP) % NQ) * (NZ * CAP) + by_z // (CAP * NQ) * CAP + by_z % CAP
    to_z_order = jnp.where(wanted == by_plane, 1.0, 0.0).astype(jnp.bfloat16)

    angles = []
    for rho in range(2):
        position = start_col + (2 * tp + rho).astype(jnp.float32)
        phase = position * freq_buf[...]
        angles.append((jnp.cos(phase), jnp.sin(phase)))

    add_and_pass(0)
    to_opposite[1] = encode(project(1, 0))
    project_right(1)
    project_left(1)

    def each_z(act):
        def step(i, carry):
            act(i + (i + NZ - z) // NZ)
            return carry

        lax.fori_loop(0, NZ - 1, step, 0)

    def z_copy(rho, other):
        return pltpu.make_async_remote_copy(
            src_ref=z_send[rho].at[other],
            dst_ref=z_recv[rho].at[z],
            send_sem=zs.at[rho, other],
            recv_sem=zr.at[rho, z],
            device_id=(z_device(other), tp),
            device_id_type=MESH,
        )

    def z_arrival(rho, other):
        return pltpu.make_async_remote_copy(
            src_ref=z_send[rho].at[other],
            dst_ref=z_recv[rho].at[other],
            send_sem=zs.at[rho, other],
            recv_sem=zr.at[rho, other],
            device_id=(z_device(other), tp),
            device_id_type=MESH,
        )

    def p_copy(rho, other):
        return pltpu.make_async_remote_copy(
            src_ref=p_send[rho].at[other],
            dst_ref=p_recv[rho].at[plane],
            send_sem=ps.at[rho, other],
            recv_sem=pr.at[rho, plane],
            device_id=(p_device(other), tp),
            device_id_type=MESH,
        )

    def p_arrival(rho, other):
        return pltpu.make_async_remote_copy(
            src_ref=p_send[rho].at[other],
            dst_ref=p_recv[rho].at[other],
            send_sem=ps.at[rho, other],
            recv_sem=pr.at[rho, other],
            device_id=(p_device(other), tp),
            device_id_type=MESH,
        )

    def each(count, me, act):
        def step(i, carry):
            act((me + i) % count)
            return carry

        lax.fori_loop(1, count, step, 0)

    def finish(rho):
        for kind in (2, 3, 4, 5):
            y_copies[rho][kind].wait_recv()
        total = part[rho, 0] + decode(from_left[rho]) + decode(from_right[rho])
        latent = total[:, :RANK]
        rotary = total[:, RANK:]
        mean_square = jnp.sum(latent * latent, axis=1, keepdims=True) * (1.0 / RANK)
        latent = latent / jnp.sqrt(mean_square + 1e-06) * gain_buf[...]
        half = (LAT - RANK) // 2
        front, back = rotary[:, :half], rotary[:, half:]
        cosine, sine = angles[rho]
        pieces = [latent, front * cosine - back * sine, back * cosine + front * sine]
        row = jnp.concatenate(pieces, axis=1)
        alive = (2 * tp + rho).astype(jnp.float32) < length_col
        row = jnp.where(alive, row, 0.0)
        if rho == 0:
            row = jnp.concatenate([row, meta], axis=1)
        return jnp.dot(
            send_tables[rho], row.astype(jnp.bfloat16), preferred_element_type=jnp.float32
        ).astype(jnp.bfloat16)

    def send_z(rho, rows):
        z_send[rho][...] = rows.reshape(z_send[rho].shape)
        z_recv[rho][z] = z_send[rho][z]
        each_z(lambda other: z_copy(rho, other).start())

    def send_p(rho, rows):
        p_send[rho][...] = rows.reshape(p_send[rho].shape)
        p_recv[rho][plane] = p_send[rho][plane]
        each(NQ, plane, lambda other: p_copy(rho, other).start())

    def arrived_z(rho):
        each_z(lambda other: z_arrival(rho, other).wait_recv())
        return z_recv[rho][...].reshape(slots, z_recv[rho].shape[-1])

    def arrived_p(rho):
        each(NQ, plane, lambda other: p_arrival(rho, other).wait_recv())
        return p_recv[rho][...].reshape(slots, p_recv[rho].shape[-1])

    def reorder(table, rows):
        return jnp.dot(table, rows, preferred_element_type=jnp.float32).astype(jnp.bfloat16)

    send_z(0, finish(0))
    start(1, 0, 1, 2, 3)
    part[1, 0] = project(1, 3)
    add_and_pass(1)
    send_p(1, finish(1))
    send_z(1, reorder(to_z_order, arrived_p(1)))
    send_p(0, reorder(to_plane_order, arrived_z(0)))
    landed = arrived_p(0)
    place = as_row(landed[:, LAT : LAT + 1].astype(jnp.float32))
    page_ids = (first_axis_iota(SEGS_EACH, slots) + 1).astype(jnp.float32)
    take_table = jnp.where(page_ids == place, 1.0, 0.0).astype(jnp.bfloat16)
    out_ref[0] = reorder(take_table, landed[:, :LAT])
    take_table = reorder(take_table, to_plane_order)
    out_ref[1] = reorder(take_table, arrived_z(1))

    for rho in range(2):
        for copy in y_copies[rho]:
            copy.wait_send()
        each_z(lambda other: z_copy(rho, other).wait_send())
        each(NQ, plane, lambda other: p_copy(rho, other).wait_send())


def shards(hidden_rows, compress_weight, latent_gain, segment_page, segment_length, segment_start):
    half = (LAT - RANK) // 2
    exponent = np.arange(half, dtype=np.float64) * (2.0 / (LAT - RANK))
    frequency = jnp.asarray(np.power(10000.0, -exponent).reshape(1, half).astype(np.float32))
    width = hidden_rows.shape[-1]
    any_spec = pl.BlockSpec(memory_space=pltpu.HBM)
    vmem_spec = pl.BlockSpec(memory_space=pltpu.VMEM)
    dma = pltpu.SemaphoreType.DMA
    bf16, f32 = jnp.bfloat16, jnp.float32
    n = SEGS_EACH
    scratch = [
        pltpu.VMEM((TP, 2, n, width), bf16),
        pltpu.VMEM((LAT, width), bf16),
        pltpu.VMEM((1, RANK), f32),
        pltpu.VMEM((n, 128), jnp.int32),
        pltpu.VMEM((n, 128), jnp.int32),
        pltpu.VMEM((n, 128), jnp.int32),
        pltpu.VMEM((1, half), f32),
        pltpu.VMEM((2, TP - 1, n, LAT), f32),
        pltpu.VMEM((2, n, WIDE), jnp.int16),
        pltpu.VMEM((2, n, WIDE), jnp.int16),
        pltpu.VMEM((2, n, WIDE), jnp.int16),
        pltpu.VMEM((2, n, WIDE), jnp.int16),
        pltpu.VMEM((2, n, WIDE), jnp.int16),
        pltpu.VMEM((2, n, WIDE), jnp.int16),
        pltpu.VMEM((NZ, NQ * CAP, WIDE), bf16),
        pltpu.VMEM((NZ, NQ * CAP, LAT), bf16),
        pltpu.VMEM((NZ, NQ * CAP, WIDE), bf16),
        pltpu.VMEM((NZ, NQ * CAP, LAT), bf16),
        pltpu.VMEM((NQ, NZ * CAP, WIDE), bf16),
        pltpu.VMEM((NQ, NZ * CAP, LAT), bf16),
        pltpu.VMEM((NQ, NZ * CAP, WIDE), bf16),
        pltpu.VMEM((NQ, NZ * CAP, LAT), bf16),
        dma((TP,)),
        dma(()),
        dma((5,)),
        dma((2, 6)),
        dma((2, 6)),
        dma((2, NZ)),
        dma((2, NZ)),
        dma((2, NQ)),
        dma((2, NQ)),
    ]
    return pl.pallas_call(
        kernel,
        out_shape=jax.ShapeDtypeStruct((2, n, LAT), bf16),
        in_specs=[any_spec] * 7,
        out_specs=vmem_spec,
        scratch_shapes=scratch,
        compiler_params=pltpu.CompilerParams(
            collective_id=0, has_side_effects=True, vmem_limit_bytes=60 * 1024 * 1024
        ),
        cost_estimate=pl.CostEstimate(
            flops=2 * 8 * n * width * LAT, bytes_accessed=7_000_000, transcendentals=0
        ),
        name="latent_rows",
    )(
        hidden_rows,
        compress_weight.T,
        latent_gain.reshape(1, RANK),
        segment_page.reshape(n, 128),
        segment_length.reshape(n, 128),
        segment_start.reshape(n, 128),
        frequency,
    )


def solution(mesh):
    in_specs = (P(None, "dec", "tp"), P("tp", None), P(), P(), P(), P())
    out_specs = P("tp", "dec", None)
    return jax.shard_map(shards, mesh=mesh, in_specs=in_specs, out_specs=out_specs, check_vma=False)
```

```python
import functools

import jax
import jax.numpy as jnp
import numpy as np
from jax import lax
from jax.experimental import pallas as pl
from jax.experimental.pallas import tpu as pltpu
from jax.sharding import PartitionSpec as P

MESH = pl.DeviceIdType.MESH
TP = 4
NZ = 16
NQ = 8
CAP = 2
SEGS_EACH = 144
RANK = 512
LAT = 576
ROT = LAT - RANK
WIDE = RANK + 2 * ROT
W_PIECES = 4
HALF_A = 80
INV_SEGS = 7282


def first_axis_iota(rows, columns):
    return lax.broadcasted_iota(jnp.int32, (rows, columns), 0)


def last_axis_iota(rows, columns):
    return lax.broadcasted_iota(jnp.int32, (rows, columns), 1)


def as_column(row):
    n = row.shape[1]
    same = first_axis_iota(n, n) == last_axis_iota(n, n)
    return jnp.sum(jnp.where(same, row, 0.0), axis=1, keepdims=True)


def as_row(column):
    n = column.shape[0]
    same = first_axis_iota(n, n) == last_axis_iota(n, n)
    return jnp.sum(jnp.where(same, column, 0.0), axis=0, keepdims=True)


def own_entries(ref, own_index):
    offset = own_index * SEGS_EACH
    top = offset // 128
    lane = offset % 128
    first = ref[pl.ds(top, 1), :]
    second = ref[pl.ds(top + 1, 1), :]
    both = jnp.concatenate([first, second], axis=1)
    rolled = pltpu.roll(both, (256 - lane) % 256, axis=1)
    return rolled[:, :SEGS_EACH]


def parts_of(block):
    edges = [0, *range(RANK, block.shape[1] + 1, ROT)]
    return [block[:, a:b] for a, b in zip(edges, edges[1:])]


def encode(block):
    n = block.shape[0]
    diagonal = first_axis_iota(n, 128) == last_axis_iota(n, 128)
    row_number = first_axis_iota(8, 128)
    scales = jnp.zeros((8, 128), jnp.float32)
    pieces = []
    for i, piece in enumerate(parts_of(block)):
        top = jnp.maximum(jnp.max(jnp.abs(piece), axis=1, keepdims=True), 1e-30)
        pieces.append(piece * (32767.0 / top))
        as_lanes = jnp.sum(jnp.where(diagonal, top, 0.0), axis=0, keepdims=True)
        scales = jnp.where(row_number == i, as_lanes, scales)
    coded = pieces[0] if len(pieces) == 1 else jnp.concatenate(pieces, axis=1)
    return jnp.round(coded).astype(jnp.int32).astype(jnp.int16), scales


def decode(coded, scales):
    block = coded.astype(jnp.int32).astype(jnp.float32)
    n = block.shape[0]
    diagonal = first_axis_iota(n, 128) == last_axis_iota(n, 128)
    pieces = []
    for i, piece in enumerate(parts_of(block)):
        top = jnp.sum(jnp.where(diagonal, scales[i : i + 1], 0.0), axis=1, keepdims=True)
        pieces.append(piece * (top * (1.0 / 32767.0)))
    return pieces[0] if len(pieces) == 1 else jnp.concatenate(pieces, axis=1)


def kernel(
    x_hbm, w_hbm, gain_hbm, page_hbm, length_hbm, start_hbm, freq_hbm, out_ref,
    x_buf, w_buf, gain_buf, page_buf, length_buf, start_buf, freq_buf,
    rotary_part, part0, part1, y_send0, y_send1, y_recv0, y_recv1, scale_send, scale_recv,
    z_send0, z_send1, z_recv0, z_recv1, p_send0, p_send1, p_recv0, p_recv1,
    x_sem, w_sem, i_sem, ys, yr, ss, sr, zs, zr, ps, pr,
):
    dec = lax.axis_index("dec")
    tp = lax.axis_index("tp")
    core = dec % 2
    z = (dec // 2) % NZ
    xx = dec // (2 * NZ)
    plane = xx * 2 + core
    left = (tp + TP - 1) % TP
    right = (tp + 1) % TP
    z_send, z_recv = (z_send0, z_send1), (z_recv0, z_recv1)
    p_send, p_recv = (p_send0, p_send1), (p_recv0, p_recv1)
    part, y_send, y_recv = (part0, part1), (y_send0, y_send1), (y_recv0, y_recv1)

    def z_device(zz):
        return xx * (2 * NZ) + zz * 2 + core

    def p_device(qq):
        return (qq // 2) * (2 * NZ) + z * 2 + qq % 2

    targets = ((tp + 2) % TP, right, left, tp)
    w_rows = LAT // W_PIECES
    w_copies = [
        pltpu.make_async_copy(
            w_hbm.at[pl.ds(i * w_rows, w_rows)], w_buf.at[pl.ds(i * w_rows, w_rows)], w_sem.at[i]
        )
        for i in range(W_PIECES)
    ]
    for copy in w_copies:
        copy.start()
    x_copies = [
        pltpu.make_async_copy(x_hbm.at[pl.ds(2 * target, 2)], x_buf.at[i], x_sem.at[i])
        for i, target in enumerate(targets)
    ]
    x_copies[0].start()
    index_copies = [
        pltpu.make_async_copy(src, dst, i_sem.at[i])
        for i, (src, dst) in enumerate(
            (
                (page_hbm, page_buf),
                (length_hbm, length_buf),
                (start_hbm, start_buf),
                (gain_hbm, gain_buf),
                (freq_hbm, freq_buf),
            )
        )
    ]
    for copy in index_copies:
        copy.start()

    barrier = pltpu.get_barrier_semaphore()
    for neighbour in (left, right):
        pl.semaphore_signal(barrier, inc=1, device_id=(dec, neighbour), device_id_type=MESH)

    def greet_z(i, carry):
        pl.semaphore_signal(
            barrier, inc=1, device_id=(z_device((z + i) % NZ), tp), device_id_type=MESH
        )
        return carry

    def greet_p(i, carry):
        pl.semaphore_signal(
            barrier, inc=1, device_id=(p_device((plane + i) % NQ), tp), device_id_type=MESH
        )
        return carry

    lax.fori_loop(1, NZ, greet_z, 0)
    lax.fori_loop(1, NQ, greet_p, 0)
    for copy in x_copies[1:]:
        copy.start()

    rows_a = pl.ds(0, HALF_A)
    rows_b = pl.ds(HALF_A, SEGS_EACH - HALF_A)

    def project(rho, i):
        result = lax.dot_general(
            x_buf[i, rho], w_buf[...], (((1,), (1,)), ((), ())), preferred_element_type=jnp.float32
        )
        if rho == 0:
            rotary_part[i] = result[:, RANK:]
            return result[:, :RANK]
        return jnp.concatenate([result[:, :RANK], rotary_part[i], result[:, RANK:]], axis=1)

    kinds = (
        (rows_a, 0, 0, right),
        (rows_b, 0, 0, left),
        (rows_b, 1, 1, right),
        (rows_a, 2, 2, left),
        (rows_a, 1, 1, right),
        (rows_b, 2, 2, left),
    )

    def y_pair(rho, kind):
        rows, source, place, target = kinds[kind]
        values = pltpu.make_async_remote_copy(
            src_ref=y_send[rho].at[source, rows],
            dst_ref=y_recv[rho].at[place, rows],
            send_sem=ys.at[rho, kind],
            recv_sem=yr.at[rho, kind],
            device_id=(dec, target),
            device_id_type=MESH,
        )
        scales = pltpu.make_async_remote_copy(
            src_ref=scale_send.at[rho, kind],
            dst_ref=scale_recv.at[rho, kind],
            send_sem=ss.at[rho, kind],
            recv_sem=sr.at[rho, kind],
            device_id=(dec, target),
            device_id_type=MESH,
        )
        return scales, values

    y_copies = [[y_pair(rho, kind) for kind in range(len(kinds))] for rho in range(2)]

    def code(rho, kind, block):
        rows, source, _, _ = kinds[kind]
        y_send[rho][source, rows], scale_send[rho, kind] = encode(block)

    def arrived_y(rho, kind):
        rows, _, place, _ = kinds[kind]
        for copy in y_copies[rho][kind]:
            copy.wait_recv()
        return decode(y_recv[rho][place, rows], scale_recv[rho, kind])

    def project_opposite(rho):
        result = project(rho, 0)
        code(rho, 0, result[:HALF_A])
        code(rho, 1, result[HALF_A:])

    def project_right(rho):
        result = project(rho, 1)
        code(rho, 2, result[HALF_A:])
        part[rho][1, rows_a] = result[:HALF_A]

    def project_left(rho):
        result = project(rho, 2)
        code(rho, 3, result[:HALF_A])
        part[rho][2, rows_b] = result[HALF_A:]

    def start(rho, *which):
        for kind in which:
            for copy in y_copies[rho][kind]:
                copy.start()

    def add_and_pass(rho):
        code(rho, 4, part[rho][1, rows_a] + arrived_y(rho, 0))
        start(rho, 4)
        code(rho, 5, part[rho][2, rows_b] + arrived_y(rho, 1))
        start(rho, 5)

    for copy in w_copies:
        copy.wait()
    x_copies[0].wait()
    project_opposite(0)
    pl.semaphore_wait(barrier, 2 + (NZ - 1) + (NQ - 1))
    start(0, 0, 1)
    x_copies[1].wait()
    project_right(0)
    x_copies[2].wait()
    project_left(0)
    start(0, 2, 3)
    x_copies[3].wait()
    part[0][0] = project(0, 3)

    for copy in index_copies:
        copy.wait()
    page_row = own_entries(page_buf, dec)
    length_row = own_entries(length_buf, dec)
    start_row = own_entries(start_buf, dec)
    owner_row = (page_row * INV_SEGS) >> 20
    length_col = as_column(length_row.astype(jnp.float32))
    start_col = as_column(start_row.astype(jnp.float32))
    owner_col = as_column(owner_row.astype(jnp.float32))
    same_owner = owner_col == owner_row.astype(jnp.float32)
    is_earlier = first_axis_iota(SEGS_EACH, SEGS_EACH) < last_axis_iota(SEGS_EACH, SEGS_EACH)
    earlier_row = jnp.sum(
        jnp.where(same_owner, jnp.where(is_earlier, 1.0, 0.0), 0.0), axis=0, keepdims=True
    ).astype(jnp.int32)
    owner_plane = (owner_row >> 5) * 2 + (owner_row & 1)
    owner_z = (owner_row >> 1) & (NZ - 1)
    slots = NZ * NQ * CAP
    slot_rows = (
        owner_z * (NQ * CAP) + owner_plane * CAP + earlier_row,
        owner_plane * (NZ * CAP) + owner_z * CAP + earlier_row,
    )
    send_tables = [
        jnp.where(first_axis_iota(slots, SEGS_EACH) == row, 1.0, 0.0).astype(jnp.bfloat16)
        for row in slot_rows
    ]

    by_plane = first_axis_iota(slots, slots)
    by_z = last_axis_iota(slots, slots)
    wanted = ((by_plane // CAP) % NZ) * (NQ * CAP) + by_plane // (CAP * NZ) * CAP + by_plane % CAP
    to_plane_order = jnp.where(wanted == by_z, 1.0, 0.0).astype(jnp.bfloat16)
    by_z, by_plane = first_axis_iota(slots, slots), last_axis_iota(slots, slots)
    wanted = ((by_z // CAP) % NQ) * (NZ * CAP) + by_z // (CAP * NQ) * CAP + by_z % CAP
    to_z_order = jnp.where(wanted == by_plane, 1.0, 0.0).astype(jnp.bfloat16)

    angles = []
    for rho in range(2):
        position = start_col + (2 * tp + rho).astype(jnp.float32)
        phase = position * freq_buf[...]
        angles.append((jnp.cos(phase), jnp.sin(phase)))

    add_and_pass(0)
    project_opposite(1)
    start(1, 0, 1)
    project_right(1)
    project_left(1)
    start(1, 2, 3)

    def each_z(act):
        def step(i, carry):
            act(i + (i + NZ - z) // NZ)
            return carry

        lax.fori_loop(0, NZ - 1, step, 0)

    def z_copy(rho, other):
        return pltpu.make_async_remote_copy(
            src_ref=z_send[rho].at[other],
            dst_ref=z_recv[rho].at[z],
            send_sem=zs.at[rho, other],
            recv_sem=zr.at[rho, z],
            device_id=(z_device(other), tp),
            device_id_type=MESH,
        )

    def z_arrival(rho, other):
        return pltpu.make_async_remote_copy(
            src_ref=z_send[rho].at[other],
            dst_ref=z_recv[rho].at[other],
            send_sem=zs.at[rho, other],
            recv_sem=zr.at[rho, other],
            device_id=(z_device(other), tp),
            device_id_type=MESH,
        )

    def p_copy(rho, other):
        return pltpu.make_async_remote_copy(
            src_ref=p_send[rho].at[other],
            dst_ref=p_recv[rho].at[plane],
            send_sem=ps.at[rho, other],
            recv_sem=pr.at[rho, plane],
            device_id=(p_device(other), tp),
            device_id_type=MESH,
        )

    def p_arrival(rho, other):
        return pltpu.make_async_remote_copy(
            src_ref=p_send[rho].at[other],
            dst_ref=p_recv[rho].at[other],
            send_sem=ps.at[rho, other],
            recv_sem=pr.at[rho, other],
            device_id=(p_device(other), tp),
            device_id_type=MESH,
        )

    def each(count, me, act):
        def step(i, carry):
            act((me + i) % count)
            return carry

        lax.fori_loop(1, count, step, 0)

    alive = [(2 * tp + rho).astype(jnp.float32) < length_col for rho in range(2)]

    def turn_rotary(rotary, rho):
        half = ROT // 2
        front, back = rotary[:, :half], rotary[:, half:]
        cosine, sine = angles[rho]
        turned = [front * cosine - back * sine, back * cosine + front * sine]
        return jnp.where(alive[rho], jnp.concatenate(turned, axis=1), 0.0)

    def finish(rho):
        total_a = part[rho][0, rows_a] + arrived_y(rho, 3) + arrived_y(rho, 4)
        total_b = part[rho][0, rows_b] + arrived_y(rho, 2) + arrived_y(rho, 5)
        total = jnp.concatenate([total_a, total_b], axis=0)
        latent = total[:, :RANK]
        mean_square = jnp.sum(latent * latent, axis=1, keepdims=True) * (1.0 / RANK)
        latent = latent / jnp.sqrt(mean_square + 1e-06) * gain_buf[...]
        row = jnp.where(alive[rho], latent, 0.0)
        if rho == 1:
            rotaries = [
                turn_rotary(total[:, RANK : RANK + ROT], 0),
                turn_rotary(total[:, RANK + ROT :], 1),
            ]
            row = jnp.concatenate([row, *rotaries], axis=1)
        return jnp.dot(
            send_tables[rho], row.astype(jnp.bfloat16), preferred_element_type=jnp.float32
        ).astype(jnp.bfloat16)

    def send_z(rho, rows):
        z_send[rho][...] = rows.reshape(z_send[rho].shape)
        z_recv[rho][z] = z_send[rho][z]
        each_z(lambda other: z_copy(rho, other).start())

    def send_p(rho, rows):
        p_send[rho][...] = rows.reshape(p_send[rho].shape)
        p_recv[rho][plane] = p_send[rho][plane]
        each(NQ, plane, lambda other: p_copy(rho, other).start())

    def arrived_z(rho):
        each_z(lambda other: z_arrival(rho, other).wait_recv())
        return z_recv[rho][...].reshape(slots, z_recv[rho].shape[-1])

    def arrived_p(rho):
        each(NQ, plane, lambda other: p_arrival(rho, other).wait_recv())
        return p_recv[rho][...].reshape(slots, p_recv[rho].shape[-1])

    def reorder(table, rows):
        return jnp.dot(table, rows, preferred_element_type=jnp.float32).astype(jnp.bfloat16)

    send_z(0, finish(0))
    add_and_pass(1)
    part[1][0] = project(1, 3)
    send_p(1, finish(1))

    own_pages = dec * SEGS_EACH + first_axis_iota(SEGS_EACH, 128)
    lane = last_axis_iota(1, 128)

    def search(i, found):
        return found + jnp.where(page_buf[pl.ds(i, 1), :] == own_pages, lane + i * 128, 0)

    found = lax.fori_loop(0, SEGS_EACH, search, jnp.zeros((SEGS_EACH, 128), jnp.int32))
    segment_col = jnp.sum(found.astype(jnp.float32), axis=1, keepdims=True)
    loader_col = (segment_col.astype(jnp.int32) * INV_SEGS) >> 20
    loader_row = as_row(loader_col.astype(jnp.float32)).astype(jnp.int32)
    is_earlier = as_row(segment_col) < segment_col
    earlier_col = jnp.sum(
        jnp.where(loader_row == loader_col, jnp.where(is_earlier, 1.0, 0.0), 0.0),
        axis=1,
        keepdims=True,
    ).astype(jnp.int32)
    loader_plane = (loader_col >> 5) * 2 + (loader_col & 1)
    loader_z = (loader_col >> 1) & (NZ - 1)
    slot = last_axis_iota(SEGS_EACH, slots)
    slot_by_plane = loader_plane * (NZ * CAP) + loader_z * CAP + earlier_col
    slot_by_z = loader_z * (NQ * CAP) + loader_plane * CAP + earlier_col
    take_by_plane = jnp.where(slot == slot_by_plane, 1.0, 0.0).astype(jnp.bfloat16)
    take_by_z = jnp.where(slot == slot_by_z, 1.0, 0.0).astype(jnp.bfloat16)

    send_z(1, reorder(to_z_order, arrived_p(1)))
    send_p(0, reorder(to_plane_order, arrived_z(0)))
    landed = arrived_p(0)
    out_ref[0, :, :RANK] = reorder(take_by_plane, landed)
    last = reorder(take_by_z, arrived_z(1))
    out_ref[0, :, RANK:] = last[:, RANK : RANK + ROT]
    out_ref[1] = jnp.concatenate([last[:, :RANK], last[:, RANK + ROT :]], axis=1)

    for rho in range(2):
        for pair in y_copies[rho]:
            for copy in pair:
                copy.wait_send()
        each_z(lambda other: z_copy(rho, other).wait_send())
        each(NQ, plane, lambda other: p_copy(rho, other).wait_send())


def shards(hidden_rows, compress_weight, latent_gain, segment_page, segment_length, segment_start):
    half = (LAT - RANK) // 2
    exponent = np.arange(half, dtype=np.float64) * (2.0 / (LAT - RANK))
    frequency = jnp.asarray(np.power(10000.0, -exponent).reshape(1, half).astype(np.float32))
    width = hidden_rows.shape[-1]
    any_spec = pl.BlockSpec(memory_space=pltpu.HBM)
    vmem_spec = pl.BlockSpec(memory_space=pltpu.VMEM)
    dma = pltpu.SemaphoreType.DMA
    bf16, f32 = jnp.bfloat16, jnp.float32
    n = SEGS_EACH
    scratch = [
        pltpu.VMEM((TP, 2, n, width), bf16),
        pltpu.VMEM((LAT, width), bf16),
        pltpu.VMEM((1, RANK), f32),
        pltpu.VMEM((n, 128), jnp.int32),
        pltpu.VMEM((n, 128), jnp.int32),
        pltpu.VMEM((n, 128), jnp.int32),
        pltpu.VMEM((1, half), f32),
        pltpu.VMEM((TP, n, ROT), f32),
        pltpu.VMEM((TP - 1, n, RANK), f32),
        pltpu.VMEM((TP - 1, n, WIDE), f32),
        pltpu.VMEM((TP - 1, n, RANK), jnp.int16),
        pltpu.VMEM((TP - 1, n, WIDE), jnp.int16),
        pltpu.VMEM((TP - 1, n, RANK), jnp.int16),
        pltpu.VMEM((TP - 1, n, WIDE), jnp.int16),
        pltpu.VMEM((2, 6, 8, 128), f32),
        pltpu.VMEM((2, 6, 8, 128), f32),
        pltpu.VMEM((NZ, NQ * CAP, RANK), bf16),
        pltpu.VMEM((NZ, NQ * CAP, WIDE), bf16),
        pltpu.VMEM((NZ, NQ * CAP, RANK), bf16),
        pltpu.VMEM((NZ, NQ * CAP, WIDE), bf16),
        pltpu.VMEM((NQ, NZ * CAP, RANK), bf16),
        pltpu.VMEM((NQ, NZ * CAP, WIDE), bf16),
        pltpu.VMEM((NQ, NZ * CAP, RANK), bf16),
        pltpu.VMEM((NQ, NZ * CAP, WIDE), bf16),
        dma((TP,)),
        dma((W_PIECES,)),
        dma((5,)),
        dma((2, 6)),
        dma((2, 6)),
        dma((2, 6)),
        dma((2, 6)),
        dma((2, NZ)),
        dma((2, NZ)),
        dma((2, NQ)),
        dma((2, NQ)),
    ]
    return pl.pallas_call(
        kernel,
        out_shape=jax.ShapeDtypeStruct((2, n, LAT), bf16),
        in_specs=[any_spec] * 7,
        out_specs=vmem_spec,
        scratch_shapes=scratch,
        compiler_params=pltpu.CompilerParams(
            collective_id=0, has_side_effects=True, vmem_limit_bytes=60 * 1024 * 1024
        ),
        cost_estimate=pl.CostEstimate(
            flops=2 * 8 * n * width * LAT, bytes_accessed=7_000_000, transcendentals=0
        ),
        name="latent_rows",
    )(
        hidden_rows,
        compress_weight.T,
        latent_gain.reshape(1, RANK),
        segment_page.reshape(n, 128),
        segment_length.reshape(n, 128),
        segment_start.reshape(n, 128),
        frequency,
    )


def solution(mesh):
    in_specs = (P(None, "dec", "tp"), P("tp", None), P(), P(), P(), P())
    out_specs = P("tp", "dec", None)
    return jax.shard_map(shards, mesh=mesh, in_specs=in_specs, out_specs=out_specs, check_vma=False)
```

```python
import functools

import jax
import jax.numpy as jnp
import numpy as np
from jax import lax
from jax.experimental import pallas as pl
from jax.experimental.pallas import tpu as pltpu
from jax.sharding import PartitionSpec as P

FIRST_PLANES = (7, 7)
MESH = pl.DeviceIdType.MESH
TP = 4
NZ = 16
NQ = 8
CAP = 2
SEGS_EACH = 144
RANK = 512
LAT = 576
ROT = LAT - RANK
WIDE = RANK + 2 * ROT
W_PIECES = 4
HALF_A = 80
INV_SEGS = 7282


def first_axis_iota(rows, columns):
    return lax.broadcasted_iota(jnp.int32, (rows, columns), 0)


def last_axis_iota(rows, columns):
    return lax.broadcasted_iota(jnp.int32, (rows, columns), 1)


def as_column(row):
    n = row.shape[1]
    same = first_axis_iota(n, n) == last_axis_iota(n, n)
    return jnp.sum(jnp.where(same, row, 0.0), axis=1, keepdims=True)


def as_row(column):
    n = column.shape[0]
    same = first_axis_iota(n, n) == last_axis_iota(n, n)
    return jnp.sum(jnp.where(same, column, 0.0), axis=0, keepdims=True)


def own_entries(ref, own_index):
    offset = own_index * SEGS_EACH
    top = offset // 128
    lane = offset % 128
    first = ref[pl.ds(top, 1), :]
    second = ref[pl.ds(top + 1, 1), :]
    both = jnp.concatenate([first, second], axis=1)
    rolled = pltpu.roll(both, (256 - lane) % 256, axis=1)
    return rolled[:, :SEGS_EACH]


def parts_of(block):
    edges = [0, *range(RANK, block.shape[1] + 1, ROT)]
    return [block[:, a:b] for a, b in zip(edges, edges[1:])]


def encode(block):
    n = block.shape[0]
    diagonal = first_axis_iota(n, 128) == last_axis_iota(n, 128)
    row_number = first_axis_iota(8, 128)
    scales = jnp.zeros((8, 128), jnp.float32)
    pieces = []
    for i, piece in enumerate(parts_of(block)):
        top = jnp.maximum(jnp.max(jnp.abs(piece), axis=1, keepdims=True), 1e-30)
        pieces.append(piece * (32767.0 / top))
        as_lanes = jnp.sum(jnp.where(diagonal, top, 0.0), axis=0, keepdims=True)
        scales = jnp.where(row_number == i, as_lanes, scales)
    coded = pieces[0] if len(pieces) == 1 else jnp.concatenate(pieces, axis=1)
    return jnp.round(coded).astype(jnp.int32).astype(jnp.int16), scales


def decode(coded, scales):
    block = coded.astype(jnp.int32).astype(jnp.float32)
    n = block.shape[0]
    diagonal = first_axis_iota(n, 128) == last_axis_iota(n, 128)
    pieces = []
    for i, piece in enumerate(parts_of(block)):
        top = jnp.sum(jnp.where(diagonal, scales[i : i + 1], 0.0), axis=1, keepdims=True)
        pieces.append(piece * (top * (1.0 / 32767.0)))
    return pieces[0] if len(pieces) == 1 else jnp.concatenate(pieces, axis=1)


def kernel(
    x_hbm, w_hbm, gain_hbm, page_hbm, length_hbm, start_hbm, freq_hbm, out_ref,
    x_buf, w_buf, gain_buf, page_buf, length_buf, start_buf, freq_buf,
    part0, part1, y_send0, y_send1, y_recv0, y_recv1, scale_send, scale_recv,
    z_send0, z_send1, z_recv0, z_recv1, p_send0, p_send1, p_recv0, p_recv1,
    x_sem, w_sem, i_sem, ys, yr, ss, sr, zs, zr, ps, pr,
):
    dec = lax.axis_index("dec")
    tp = lax.axis_index("tp")
    core = dec % 2
    z = (dec // 2) % NZ
    xx = dec // (2 * NZ)
    plane = xx * 2 + core
    left = (tp + TP - 1) % TP
    right = (tp + 1) % TP
    z_send, z_recv = (z_send0, z_send1), (z_recv0, z_recv1)
    p_send, p_recv = (p_send0, p_send1), (p_recv0, p_recv1)
    part, y_send, y_recv = (part0, part1), (y_send0, y_send1), (y_recv0, y_recv1)

    def z_device(zz):
        return xx * (2 * NZ) + zz * 2 + core

    def p_device(qq):
        return (qq // 2) * (2 * NZ) + z * 2 + qq % 2

    targets = ((tp + 2) % TP, right, left, tp)
    w_rows = LAT // W_PIECES
    w_copies = [
        pltpu.make_async_copy(
            w_hbm.at[pl.ds(i * w_rows, w_rows)], w_buf.at[pl.ds(i * w_rows, w_rows)], w_sem.at[i]
        )
        for i in range(W_PIECES)
    ]
    for copy in w_copies:
        copy.start()
    x_copies = [
        pltpu.make_async_copy(x_hbm.at[pl.ds(2 * target, 2)], x_buf.at[i], x_sem.at[i])
        for i, target in enumerate(targets)
    ]
    x_copies[0].start()
    index_copies = [
        pltpu.make_async_copy(src, dst, i_sem.at[i])
        for i, (src, dst) in enumerate(
            (
                (page_hbm, page_buf),
                (length_hbm, length_buf),
                (start_hbm, start_buf),
                (gain_hbm, gain_buf),
                (freq_hbm, freq_buf),
            )
        )
    ]
    for copy in index_copies:
        copy.start()

    barrier = pltpu.get_barrier_semaphore()
    for neighbour in (left, right):
        pl.semaphore_signal(barrier, inc=1, device_id=(dec, neighbour), device_id_type=MESH)

    def greet_z(i, carry):
        pl.semaphore_signal(
            barrier, inc=1, device_id=(z_device((z + i) % NZ), tp), device_id_type=MESH
        )
        return carry

    def greet_p(i, carry):
        pl.semaphore_signal(
            barrier, inc=1, device_id=(p_device((plane + i) % NQ), tp), device_id_type=MESH
        )
        return carry

    lax.fori_loop(1, NZ, greet_z, 0)
    lax.fori_loop(1, NQ, greet_p, 0)
    for copy in x_copies[1:]:
        copy.start()

    rows_a = pl.ds(0, HALF_A)
    rows_b = pl.ds(HALF_A, SEGS_EACH - HALF_A)

    def times_weight(rows, first, last):
        return lax.dot_general(
            rows, w_buf[first:last], (((1,), (1,)), ((), ())), preferred_element_type=jnp.float32
        )

    def project(rho, i):
        latent = times_weight(x_buf[i, rho], 0, RANK)
        if rho == 1:
            return latent
        both = x_buf[i].reshape(2 * SEGS_EACH, x_buf.shape[-1])
        rotary = times_weight(both, RANK, LAT)
        return jnp.concatenate([latent, rotary[:SEGS_EACH], rotary[SEGS_EACH:]], axis=1)

    kinds = (
        (rows_a, 0, 0, right),
        (rows_b, 0, 0, left),
        (rows_b, 1, 1, right),
        (rows_a, 2, 2, left),
        (rows_a, 1, 1, right),
        (rows_b, 2, 2, left),
    )

    def y_pair(rho, kind):
        rows, source, place, target = kinds[kind]
        values = pltpu.make_async_remote_copy(
            src_ref=y_send[rho].at[source, rows],
            dst_ref=y_recv[rho].at[place, rows],
            send_sem=ys.at[rho, kind],
            recv_sem=yr.at[rho, kind],
            device_id=(dec, target),
            device_id_type=MESH,
        )
        scales = pltpu.make_async_remote_copy(
            src_ref=scale_send.at[rho, kind],
            dst_ref=scale_recv.at[rho, kind],
            send_sem=ss.at[rho, kind],
            recv_sem=sr.at[rho, kind],
            device_id=(dec, target),
            device_id_type=MESH,
        )
        return scales, values

    y_copies = [[y_pair(rho, kind) for kind in range(len(kinds))] for rho in range(2)]

    def code(rho, kind, block):
        rows, source, _, _ = kinds[kind]
        y_send[rho][source, rows], scale_send[rho, kind] = encode(block)

    def arrived_y(rho, kind):
        rows, _, place, _ = kinds[kind]
        for copy in y_copies[rho][kind]:
            copy.wait_recv()
        return decode(y_recv[rho][place, rows], scale_recv[rho, kind])

    def project_opposite(rho):
        result = project(rho, 0)
        code(rho, 0, result[:HALF_A])
        code(rho, 1, result[HALF_A:])

    def project_right(rho):
        result = project(rho, 1)
        code(rho, 2, result[HALF_A:])
        part[rho][1, rows_a] = result[:HALF_A]

    def project_left(rho):
        result = project(rho, 2)
        code(rho, 3, result[:HALF_A])
        part[rho][2, rows_b] = result[HALF_A:]

    def start(rho, *which):
        for kind in which:
            for copy in y_copies[rho][kind]:
                copy.start()

    def add_and_pass(rho):
        code(rho, 4, part[rho][1, rows_a] + arrived_y(rho, 0))
        start(rho, 4)
        code(rho, 5, part[rho][2, rows_b] + arrived_y(rho, 1))
        start(rho, 5)

    for copy in w_copies:
        copy.wait()
    x_copies[0].wait()
    project_opposite(0)
    pl.semaphore_wait(barrier, 2 + (NZ - 1) + (NQ - 1))
    start(0, 0, 1)
    x_copies[1].wait()
    project_right(0)
    x_copies[2].wait()
    project_left(0)
    start(0, 2, 3)
    x_copies[3].wait()
    part[0][0] = project(0, 3)

    for copy in index_copies:
        copy.wait()
    page_row = own_entries(page_buf, dec)
    length_row = own_entries(length_buf, dec)
    start_row = own_entries(start_buf, dec)
    owner_row = (page_row * INV_SEGS) >> 20
    length_col = as_column(length_row.astype(jnp.float32))
    start_col = as_column(start_row.astype(jnp.float32))
    owner_col = as_column(owner_row.astype(jnp.float32))
    same_owner = owner_col == owner_row.astype(jnp.float32)
    is_earlier = first_axis_iota(SEGS_EACH, SEGS_EACH) < last_axis_iota(SEGS_EACH, SEGS_EACH)
    earlier_row = jnp.sum(
        jnp.where(same_owner, jnp.where(is_earlier, 1.0, 0.0), 0.0), axis=0, keepdims=True
    ).astype(jnp.int32)
    owner_plane = (owner_row >> 5) * 2 + (owner_row & 1)
    owner_z = (owner_row >> 1) & (NZ - 1)
    slots = NZ * NQ * CAP
    slot_rows = (
        owner_z * (NQ * CAP) + owner_plane * CAP + earlier_row,
        owner_plane * (NZ * CAP) + owner_z * CAP + earlier_row,
    )
    send_tables = [
        jnp.where(first_axis_iota(slots, SEGS_EACH) == row, 1.0, 0.0).astype(jnp.bfloat16)
        for row in slot_rows
    ]

    by_plane = first_axis_iota(slots, slots)
    by_z = last_axis_iota(slots, slots)
    wanted = ((by_plane // CAP) % NZ) * (NQ * CAP) + by_plane // (CAP * NZ) * CAP + by_plane % CAP
    to_plane_order = jnp.where(wanted == by_z, 1.0, 0.0).astype(jnp.bfloat16)
    by_z, by_plane = first_axis_iota(slots, slots), last_axis_iota(slots, slots)
    wanted = ((by_z // CAP) % NQ) * (NZ * CAP) + by_z // (CAP * NQ) * CAP + by_z % CAP
    to_z_order = jnp.where(wanted == by_plane, 1.0, 0.0).astype(jnp.bfloat16)

    angles = []
    for rho in range(2):
        position = start_col + (2 * tp + rho).astype(jnp.float32)
        phase = position * freq_buf[...]
        angles.append((jnp.cos(phase), jnp.sin(phase)))

    add_and_pass(0)
    project_opposite(1)
    start(1, 0, 1)
    project_right(1)
    project_left(1)
    start(1, 2, 3)

    def each_z(act):
        def step(i, carry):
            act(i + (i + NZ - z) // NZ)
            return carry

        lax.fori_loop(0, NZ - 1, step, 0)

    def far_z(first, act):
        def ahead(i, carry):
            @pl.when(z != i)
            def _():
                act(i)

            return carry

        def others(i, carry):
            other = (z + NZ // 2 + (1 - 2 * (i % 2)) * ((i + 1) // 2) + NZ) % NZ

            @pl.when(other >= first)
            def _():
                act(other)

            return carry

        lax.fori_loop(0, first, ahead, 0)
        lax.fori_loop(0, NZ - 1, others, 0)

    def z_copy(rho, other):
        return pltpu.make_async_remote_copy(
            src_ref=z_send[rho].at[other],
            dst_ref=z_recv[rho].at[z],
            send_sem=zs.at[rho, other],
            recv_sem=zr.at[rho, z],
            device_id=(z_device(other), tp),
            device_id_type=MESH,
        )

    def z_arrival(rho, other):
        return pltpu.make_async_remote_copy(
            src_ref=z_send[rho].at[other],
            dst_ref=z_recv[rho].at[other],
            send_sem=zs.at[rho, other],
            recv_sem=zr.at[rho, other],
            device_id=(z_device(other), tp),
            device_id_type=MESH,
        )

    def p_copy(rho, other):
        return pltpu.make_async_remote_copy(
            src_ref=p_send[rho].at[other],
            dst_ref=p_recv[rho].at[plane],
            send_sem=ps.at[rho, other],
            recv_sem=pr.at[rho, plane],
            device_id=(p_device(other), tp),
            device_id_type=MESH,
        )

    def p_arrival(rho, other):
        return pltpu.make_async_remote_copy(
            src_ref=p_send[rho].at[other],
            dst_ref=p_recv[rho].at[other],
            send_sem=ps.at[rho, other],
            recv_sem=pr.at[rho, other],
            device_id=(p_device(other), tp),
            device_id_type=MESH,
        )

    def each(count, me, act):
        def step(i, carry):
            act((me + i) % count)
            return carry

        lax.fori_loop(1, count, step, 0)

    alive = [(2 * tp + rho).astype(jnp.float32) < length_col for rho in range(2)]

    def turn_rotary(rotary, rho):
        half = ROT // 2
        front, back = rotary[:, :half], rotary[:, half:]
        cosine, sine = angles[rho]
        turned = [front * cosine - back * sine, back * cosine + front * sine]
        return jnp.where(alive[rho], jnp.concatenate(turned, axis=1), 0.0)

    def finish(rho):
        total_a = part[rho][0, rows_a] + arrived_y(rho, 3) + arrived_y(rho, 4)
        total_b = part[rho][0, rows_b] + arrived_y(rho, 2) + arrived_y(rho, 5)
        total = jnp.concatenate([total_a, total_b], axis=0)
        latent = total[:, :RANK]
        mean_square = jnp.sum(latent * latent, axis=1, keepdims=True) * (1.0 / RANK)
        latent = latent / jnp.sqrt(mean_square + 1e-06) * gain_buf[...]
        row = jnp.where(alive[rho], latent, 0.0)
        if rho == 0:
            rotaries = [
                turn_rotary(total[:, RANK : RANK + ROT], 0),
                turn_rotary(total[:, RANK + ROT :], 1),
            ]
            row = jnp.concatenate([row, *rotaries], axis=1)
        return jnp.dot(
            send_tables[rho], row.astype(jnp.bfloat16), preferred_element_type=jnp.float32
        ).astype(jnp.bfloat16)

    def send_z(rho, rows):
        z_send[rho][...] = rows.reshape(z_send[rho].shape)
        z_recv[rho][z] = z_send[rho][z]
        far_z(FIRST_PLANES[rho], lambda other: z_copy(rho, other).start())

    def send_p(rho, rows):
        p_send[rho][...] = rows.reshape(p_send[rho].shape)
        p_recv[rho][plane] = p_send[rho][plane]
        each(NQ, plane, lambda other: p_copy(rho, other).start())

    def arrived_z(rho):
        each_z(lambda other: z_arrival(rho, other).wait_recv())
        return z_recv[rho][...].reshape(slots, z_recv[rho].shape[-1])

    def arrived_p(rho):
        each(NQ, plane, lambda other: p_arrival(rho, other).wait_recv())
        return p_recv[rho][...].reshape(slots, p_recv[rho].shape[-1])

    def reorder(table, rows):
        return jnp.dot(table, rows, preferred_element_type=jnp.float32).astype(jnp.bfloat16)

    send_z(0, finish(0))
    add_and_pass(1)
    part[1][0] = project(1, 3)
    send_p(1, finish(1))

    own_pages = dec * SEGS_EACH + first_axis_iota(SEGS_EACH, 128)
    lane = last_axis_iota(1, 128)

    def search(i, found):
        return found + jnp.where(page_buf[pl.ds(i, 1), :] == own_pages, lane + i * 128, 0)

    found = lax.fori_loop(0, SEGS_EACH, search, jnp.zeros((SEGS_EACH, 128), jnp.int32))
    segment_col = jnp.sum(found.astype(jnp.float32), axis=1, keepdims=True)
    loader_col = (segment_col.astype(jnp.int32) * INV_SEGS) >> 20
    loader_row = as_row(loader_col.astype(jnp.float32)).astype(jnp.int32)
    is_earlier = as_row(segment_col) < segment_col
    earlier_col = jnp.sum(
        jnp.where(loader_row == loader_col, jnp.where(is_earlier, 1.0, 0.0), 0.0),
        axis=1,
        keepdims=True,
    ).astype(jnp.int32)
    loader_plane = (loader_col >> 5) * 2 + (loader_col & 1)
    loader_z = (loader_col >> 1) & (NZ - 1)
    slot = last_axis_iota(SEGS_EACH, slots)
    slot_by_plane = loader_plane * (NZ * CAP) + loader_z * CAP + earlier_col
    slot_by_z = loader_z * (NQ * CAP) + loader_plane * CAP + earlier_col
    take_by_plane = jnp.where(slot == slot_by_plane, 1.0, 0.0).astype(jnp.bfloat16)
    take_by_z = jnp.where(slot == slot_by_z, 1.0, 0.0).astype(jnp.bfloat16)

    send_z(1, reorder(to_z_order, arrived_p(1)))
    send_p(0, reorder(to_plane_order, arrived_z(0)))
    landed = arrived_p(0)
    first = reorder(take_by_plane, landed)
    out_ref[0] = first[:, :LAT]
    out_ref[1, :, RANK:] = first[:, LAT:]
    out_ref[1, :, :RANK] = reorder(take_by_z, arrived_z(1))

    for rho in range(2):
        for pair in y_copies[rho]:
            for copy in pair:
                copy.wait_send()
        each_z(lambda other: z_copy(rho, other).wait_send())
        each(NQ, plane, lambda other: p_copy(rho, other).wait_send())


def shards(hidden_rows, compress_weight, latent_gain, segment_page, segment_length, segment_start):
    half = (LAT - RANK) // 2
    exponent = np.arange(half, dtype=np.float64) * (2.0 / (LAT - RANK))
    frequency = jnp.asarray(np.power(10000.0, -exponent).reshape(1, half).astype(np.float32))
    width = hidden_rows.shape[-1]
    any_spec = pl.BlockSpec(memory_space=pltpu.HBM)
    vmem_spec = pl.BlockSpec(memory_space=pltpu.VMEM)
    dma = pltpu.SemaphoreType.DMA
    bf16, f32 = jnp.bfloat16, jnp.float32
    n = SEGS_EACH
    scratch = [
        pltpu.VMEM((TP, 2, n, width), bf16),
        pltpu.VMEM((LAT, width), bf16),
        pltpu.VMEM((1, RANK), f32),
        pltpu.VMEM((n, 128), jnp.int32),
        pltpu.VMEM((n, 128), jnp.int32),
        pltpu.VMEM((n, 128), jnp.int32),
        pltpu.VMEM((1, half), f32),
        pltpu.VMEM((TP - 1, n, WIDE), f32),
        pltpu.VMEM((TP - 1, n, RANK), f32),
        pltpu.VMEM((TP - 1, n, WIDE), jnp.int16),
        pltpu.VMEM((TP - 1, n, RANK), jnp.int16),
        pltpu.VMEM((TP - 1, n, WIDE), jnp.int16),
        pltpu.VMEM((TP - 1, n, RANK), jnp.int16),
        pltpu.VMEM((2, 6, 8, 128), f32),
        pltpu.VMEM((2, 6, 8, 128), f32),
        pltpu.VMEM((NZ, NQ * CAP, WIDE), bf16),
        pltpu.VMEM((NZ, NQ * CAP, RANK), bf16),
        pltpu.VMEM((NZ, NQ * CAP, WIDE), bf16),
        pltpu.VMEM((NZ, NQ * CAP, RANK), bf16),
        pltpu.VMEM((NQ, NZ * CAP, WIDE), bf16),
        pltpu.VMEM((NQ, NZ * CAP, RANK), bf16),
        pltpu.VMEM((NQ, NZ * CAP, WIDE), bf16),
        pltpu.VMEM((NQ, NZ * CAP, RANK), bf16),
        dma((TP,)),
        dma((W_PIECES,)),
        dma((5,)),
        dma((2, 6)),
        dma((2, 6)),
        dma((2, 6)),
        dma((2, 6)),
        dma((2, NZ)),
        dma((2, NZ)),
        dma((2, NQ)),
        dma((2, NQ)),
    ]
    return pl.pallas_call(
        kernel,
        out_shape=jax.ShapeDtypeStruct((2, n, LAT), bf16),
        in_specs=[any_spec] * 7,
        out_specs=vmem_spec,
        scratch_shapes=scratch,
        compiler_params=pltpu.CompilerParams(
            collective_id=0, has_side_effects=True, vmem_limit_bytes=60 * 1024 * 1024
        ),
        cost_estimate=pl.CostEstimate(
            flops=2 * 8 * n * width * LAT, bytes_accessed=7_000_000, transcendentals=0
        ),
        name="latent_rows",
    )(
        hidden_rows,
        compress_weight.T,
        latent_gain.reshape(1, RANK),
        segment_page.reshape(n, 128),
        segment_length.reshape(n, 128),
        segment_start.reshape(n, 128),
        frequency,
    )


def solution(mesh):
    in_specs = (P(None, "dec", "tp"), P("tp", None), P(), P(), P(), P())
    out_specs = P("tp", "dec", None)
    return jax.shard_map(shards, mesh=mesh, in_specs=in_specs, out_specs=out_specs, check_vma=False)
```

```python
import functools

import jax
import jax.numpy as jnp
import numpy as np
from jax import lax
from jax.experimental import pallas as pl
from jax.experimental.pallas import tpu as pltpu
from jax.sharding import PartitionSpec as P

FIRST_PLANES = (7, 7)
MESH = pl.DeviceIdType.MESH
TP = 4
NZ = 16
NQ = 8
CAP = 2
SEGS_EACH = 144
RANK = 512
LAT = 576
ROT = LAT - RANK
WIDE = RANK + 2 * ROT
W_PIECES = 4
HALF_A = 80
INV_SEGS = 7282


def first_axis_iota(rows, columns):
    return lax.broadcasted_iota(jnp.int32, (rows, columns), 0)


def last_axis_iota(rows, columns):
    return lax.broadcasted_iota(jnp.int32, (rows, columns), 1)


def as_column(row):
    n = row.shape[1]
    same = first_axis_iota(n, n) == last_axis_iota(n, n)
    return jnp.sum(jnp.where(same, row, 0.0), axis=1, keepdims=True)


def as_row(column):
    n = column.shape[0]
    same = first_axis_iota(n, n) == last_axis_iota(n, n)
    return jnp.sum(jnp.where(same, column, 0.0), axis=0, keepdims=True)


def own_entries(ref, own_index):
    offset = own_index * SEGS_EACH
    top = offset // 128
    lane = offset % 128
    first = ref[pl.ds(top, 1), :]
    second = ref[pl.ds(top + 1, 1), :]
    both = jnp.concatenate([first, second], axis=1)
    rolled = pltpu.roll(both, (256 - lane) % 256, axis=1)
    return rolled[:, :SEGS_EACH]


def parts_of(block):
    edges = [0, *range(RANK, block.shape[1] + 1, ROT)]
    return [block[:, a:b] for a, b in zip(edges, edges[1:])]


def encode(block):
    n = block.shape[0]
    diagonal = first_axis_iota(n, 128) == last_axis_iota(n, 128)
    row_number = first_axis_iota(8, 128)
    scales = jnp.zeros((8, 128), jnp.float32)
    pieces = []
    for i, piece in enumerate(parts_of(block)):
        top = jnp.maximum(jnp.max(jnp.abs(piece), axis=1, keepdims=True), 1e-30)
        pieces.append(piece * (32767.0 / top))
        as_lanes = jnp.sum(jnp.where(diagonal, top, 0.0), axis=0, keepdims=True)
        scales = jnp.where(row_number == i, as_lanes, scales)
    coded = pieces[0] if len(pieces) == 1 else jnp.concatenate(pieces, axis=1)
    return jnp.round(coded).astype(jnp.int32).astype(jnp.int16), scales


def decode(coded, scales):
    block = coded.astype(jnp.int32).astype(jnp.float32)
    n = block.shape[0]
    diagonal = first_axis_iota(n, 128) == last_axis_iota(n, 128)
    pieces = []
    for i, piece in enumerate(parts_of(block)):
        top = jnp.sum(jnp.where(diagonal, scales[i : i + 1], 0.0), axis=1, keepdims=True)
        pieces.append(piece * (top * (1.0 / 32767.0)))
    return pieces[0] if len(pieces) == 1 else jnp.concatenate(pieces, axis=1)


def kernel(
    x_hbm, w_hbm, gain_hbm, page_hbm, length_hbm, start_hbm, freq_hbm, out_hbm,
    x_buf, w_buf, gain_buf, page_buf, length_buf, start_buf, freq_buf,
    part0, part1, y_send0, y_send1, y_recv0, y_recv1, scale_send, scale_recv,
    z_send0, z_send1, z_recv0, z_recv1, p_send0, p_send1, p_recv0, p_recv1, out_buf,
    x_sem, w_sem, i_sem, ys, yr, ss, sr, zs, zr, ps, pr, o_sem,
):
    dec = lax.axis_index("dec")
    tp = lax.axis_index("tp")
    core = dec % 2
    z = (dec // 2) % NZ
    xx = dec // (2 * NZ)
    plane = xx * 2 + core
    left = (tp + TP - 1) % TP
    right = (tp + 1) % TP
    z_send, z_recv = (z_send0, z_send1), (z_recv0, z_recv1)
    p_send, p_recv = (p_send0, p_send1), (p_recv0, p_recv1)
    part, y_send, y_recv = (part0, part1), (y_send0, y_send1), (y_recv0, y_recv1)

    def z_device(zz):
        return xx * (2 * NZ) + zz * 2 + core

    def p_device(qq):
        return (qq // 2) * (2 * NZ) + z * 2 + qq % 2

    targets = ((tp + 2) % TP, right, left, tp)
    w_rows = LAT // W_PIECES
    w_copies = [
        pltpu.make_async_copy(
            w_hbm.at[pl.ds(i * w_rows, w_rows)], w_buf.at[pl.ds(i * w_rows, w_rows)], w_sem.at[i]
        )
        for i in range(W_PIECES)
    ]
    for copy in w_copies:
        copy.start()
    x_copies = [
        pltpu.make_async_copy(x_hbm.at[pl.ds(2 * target, 2)], x_buf.at[i], x_sem.at[i])
        for i, target in enumerate(targets)
    ]
    x_copies[0].start()
    index_copies = [
        pltpu.make_async_copy(src, dst, i_sem.at[i])
        for i, (src, dst) in enumerate(
            (
                (page_hbm, page_buf),
                (length_hbm, length_buf),
                (start_hbm, start_buf),
                (gain_hbm, gain_buf),
                (freq_hbm, freq_buf),
            )
        )
    ]
    for copy in index_copies:
        copy.start()

    barrier = pltpu.get_barrier_semaphore()
    for neighbour in (left, right):
        pl.semaphore_signal(barrier, inc=1, device_id=(dec, neighbour), device_id_type=MESH)

    def greet_z(i, carry):
        pl.semaphore_signal(
            barrier, inc=1, device_id=(z_device((z + i) % NZ), tp), device_id_type=MESH
        )
        return carry

    def greet_p(i, carry):
        pl.semaphore_signal(
            barrier, inc=1, device_id=(p_device((plane + i) % NQ), tp), device_id_type=MESH
        )
        return carry

    lax.fori_loop(1, NZ, greet_z, 0)
    lax.fori_loop(1, NQ, greet_p, 0)
    for copy in x_copies[1:]:
        copy.start()

    rows_a = pl.ds(0, HALF_A)
    rows_b = pl.ds(HALF_A, SEGS_EACH - HALF_A)

    def times_weight(rows, first, last):
        return lax.dot_general(
            rows, w_buf[first:last], (((1,), (1,)), ((), ())), preferred_element_type=jnp.float32
        )

    def project(rho, i):
        latent = times_weight(x_buf[i, rho], 0, RANK)
        if rho == 1:
            return latent
        both = x_buf[i].reshape(2 * SEGS_EACH, x_buf.shape[-1])
        rotary = times_weight(both, RANK, LAT)
        return jnp.concatenate([latent, rotary[:SEGS_EACH], rotary[SEGS_EACH:]], axis=1)

    kinds = (
        (rows_a, 0, 0, right),
        (rows_b, 0, 0, left),
        (rows_b, 1, 1, right),
        (rows_a, 2, 2, left),
        (rows_a, 1, 1, right),
        (rows_b, 2, 2, left),
    )

    def y_pair(rho, kind):
        rows, source, place, target = kinds[kind]
        values = pltpu.make_async_remote_copy(
            src_ref=y_send[rho].at[source, rows],
            dst_ref=y_recv[rho].at[place, rows],
            send_sem=ys.at[rho, kind],
            recv_sem=yr.at[rho, kind],
            device_id=(dec, target),
            device_id_type=MESH,
        )
        scales = pltpu.make_async_remote_copy(
            src_ref=scale_send.at[rho, kind],
            dst_ref=scale_recv.at[rho, kind],
            send_sem=ss.at[rho, kind],
            recv_sem=sr.at[rho, kind],
            device_id=(dec, target),
            device_id_type=MESH,
        )
        return scales, values

    y_copies = [[y_pair(rho, kind) for kind in range(len(kinds))] for rho in range(2)]

    def code(rho, kind, block):
        rows, source, _, _ = kinds[kind]
        y_send[rho][source, rows], scale_send[rho, kind] = encode(block)

    def arrived_y(rho, kind):
        rows, _, place, _ = kinds[kind]
        for copy in y_copies[rho][kind]:
            copy.wait_recv()
        return decode(y_recv[rho][place, rows], scale_recv[rho, kind])

    def start(rho, *which):
        for kind in which:
            for copy in y_copies[rho][kind]:
                copy.start()

    def project_opposite(rho):
        result = project(rho, 0)
        code(rho, 0, result[:HALF_A])
        if rho == 0:
            pl.semaphore_wait(barrier, 2 + (NZ - 1) + (NQ - 1))
        start(rho, 0)
        code(rho, 1, result[HALF_A:])
        start(rho, 1)

    def project_right(rho):
        result = project(rho, 1)
        code(rho, 2, result[HALF_A:])
        part[rho][1, rows_a] = result[:HALF_A]

    def project_left(rho):
        result = project(rho, 2)
        code(rho, 3, result[:HALF_A])
        part[rho][2, rows_b] = result[HALF_A:]

    def add_and_pass(rho):
        code(rho, 4, part[rho][1, rows_a] + arrived_y(rho, 0))
        start(rho, 4)
        code(rho, 5, part[rho][2, rows_b] + arrived_y(rho, 1))
        start(rho, 5)

    for copy in w_copies:
        copy.wait()
    x_copies[0].wait()
    project_opposite(0)
    x_copies[1].wait()
    project_right(0)
    x_copies[2].wait()
    project_left(0)
    start(0, 2, 3)
    x_copies[3].wait()
    part[0][0] = project(0, 3)

    for copy in index_copies:
        copy.wait()
    page_row = own_entries(page_buf, dec)
    length_row = own_entries(length_buf, dec)
    start_row = own_entries(start_buf, dec)
    owner_row = (page_row * INV_SEGS) >> 20
    length_col = as_column(length_row.astype(jnp.float32))
    start_col = as_column(start_row.astype(jnp.float32))
    owner_col = as_column(owner_row.astype(jnp.float32))
    same_owner = owner_col == owner_row.astype(jnp.float32)
    is_earlier = first_axis_iota(SEGS_EACH, SEGS_EACH) < last_axis_iota(SEGS_EACH, SEGS_EACH)
    earlier_row = jnp.sum(
        jnp.where(same_owner, jnp.where(is_earlier, 1.0, 0.0), 0.0), axis=0, keepdims=True
    ).astype(jnp.int32)
    owner_plane = (owner_row >> 5) * 2 + (owner_row & 1)
    owner_z = (owner_row >> 1) & (NZ - 1)
    slots = NZ * NQ * CAP
    slot_rows = (
        owner_z * (NQ * CAP) + owner_plane * CAP + earlier_row,
        owner_plane * (NZ * CAP) + owner_z * CAP + earlier_row,
    )
    send_tables = [
        jnp.where(first_axis_iota(slots, SEGS_EACH) == row, 1.0, 0.0).astype(jnp.bfloat16)
        for row in slot_rows
    ]

    by_plane = first_axis_iota(slots, slots)
    by_z = last_axis_iota(slots, slots)
    wanted = ((by_plane // CAP) % NZ) * (NQ * CAP) + by_plane // (CAP * NZ) * CAP + by_plane % CAP
    to_plane_order = jnp.where(wanted == by_z, 1.0, 0.0).astype(jnp.bfloat16)
    by_z, by_plane = first_axis_iota(slots, slots), last_axis_iota(slots, slots)
    wanted = ((by_z // CAP) % NQ) * (NZ * CAP) + by_z // (CAP * NQ) * CAP + by_z % CAP
    to_z_order = jnp.where(wanted == by_plane, 1.0, 0.0).astype(jnp.bfloat16)

    angles = []
    for rho in range(2):
        position = start_col + (2 * tp + rho).astype(jnp.float32)
        phase = position * freq_buf[...]
        angles.append((jnp.cos(phase), jnp.sin(phase)))

    add_and_pass(0)
    project_opposite(1)
    project_right(1)
    project_left(1)
    start(1, 2, 3)

    def each_z(act):
        def step(i, carry):
            act(i + (i + NZ - z) // NZ)
            return carry

        lax.fori_loop(0, NZ - 1, step, 0)

    def far_z(first, act):
        def ahead(i, carry):
            @pl.when(z != i)
            def _():
                act(i)

            return carry

        def others(i, carry):
            other = (z + NZ // 2 + (1 - 2 * (i % 2)) * ((i + 1) // 2) + NZ) % NZ

            @pl.when(other >= first)
            def _():
                act(other)

            return carry

        lax.fori_loop(0, first, ahead, 0)
        lax.fori_loop(0, NZ - 1, others, 0)

    def z_copy(rho, other):
        return pltpu.make_async_remote_copy(
            src_ref=z_send[rho].at[other],
            dst_ref=z_recv[rho].at[z],
            send_sem=zs.at[rho, other],
            recv_sem=zr.at[rho, z],
            device_id=(z_device(other), tp),
            device_id_type=MESH,
        )

    def z_arrival(rho, other):
        return pltpu.make_async_remote_copy(
            src_ref=z_send[rho].at[other],
            dst_ref=z_recv[rho].at[other],
            send_sem=zs.at[rho, other],
            recv_sem=zr.at[rho, other],
            device_id=(z_device(other), tp),
            device_id_type=MESH,
        )

    def p_copy(rho, other):
        return pltpu.make_async_remote_copy(
            src_ref=p_send[rho].at[other],
            dst_ref=p_recv[rho].at[plane],
            send_sem=ps.at[rho, other],
            recv_sem=pr.at[rho, plane],
            device_id=(p_device(other), tp),
            device_id_type=MESH,
        )

    def p_arrival(rho, other):
        return pltpu.make_async_remote_copy(
            src_ref=p_send[rho].at[other],
            dst_ref=p_recv[rho].at[other],
            send_sem=ps.at[rho, other],
            recv_sem=pr.at[rho, other],
            device_id=(p_device(other), tp),
            device_id_type=MESH,
        )

    def each(count, me, act):
        def step(i, carry):
            act((me + i) % count)
            return carry

        lax.fori_loop(1, count, step, 0)

    alive = [(2 * tp + rho).astype(jnp.float32) < length_col for rho in range(2)]

    def turn_rotary(rotary, rho):
        half = ROT // 2
        front, back = rotary[:, :half], rotary[:, half:]
        cosine, sine = angles[rho]
        turned = [front * cosine - back * sine, back * cosine + front * sine]
        return jnp.where(alive[rho], jnp.concatenate(turned, axis=1), 0.0)

    def finish(rho):
        total_a = part[rho][0, rows_a] + arrived_y(rho, 3) + arrived_y(rho, 4)
        total_b = part[rho][0, rows_b] + arrived_y(rho, 2) + arrived_y(rho, 5)
        total = jnp.concatenate([total_a, total_b], axis=0)
        latent = total[:, :RANK]
        mean_square = jnp.sum(latent * latent, axis=1, keepdims=True) * (1.0 / RANK)
        latent = latent / jnp.sqrt(mean_square + 1e-06) * gain_buf[...]
        row = jnp.where(alive[rho], latent, 0.0)
        if rho == 0:
            rotaries = [
                turn_rotary(total[:, RANK : RANK + ROT], 0),
                turn_rotary(total[:, RANK + ROT :], 1),
            ]
            row = jnp.concatenate([row, *rotaries], axis=1)
        return jnp.dot(
            send_tables[rho], row.astype(jnp.bfloat16), preferred_element_type=jnp.float32
        ).astype(jnp.bfloat16)

    def send_z(rho, rows):
        z_send[rho][...] = rows.reshape(z_send[rho].shape)
        z_recv[rho][z] = z_send[rho][z]
        far_z(FIRST_PLANES[rho], lambda other: z_copy(rho, other).start())

    def send_p(rho, rows):
        p_send[rho][...] = rows.reshape(p_send[rho].shape)
        p_recv[rho][plane] = p_send[rho][plane]
        each(NQ, plane, lambda other: p_copy(rho, other).start())

    def arrived_z(rho):
        each_z(lambda other: z_arrival(rho, other).wait_recv())
        return z_recv[rho][...].reshape(slots, z_recv[rho].shape[-1])

    def arrived_p(rho):
        each(NQ, plane, lambda other: p_arrival(rho, other).wait_recv())
        return p_recv[rho][...].reshape(slots, p_recv[rho].shape[-1])

    def reorder(table, rows):
        return jnp.dot(table, rows, preferred_element_type=jnp.float32).astype(jnp.bfloat16)

    send_z(0, finish(0))
    add_and_pass(1)
    part[1][0] = project(1, 3)
    send_p(1, finish(1))

    own_pages = dec * SEGS_EACH + first_axis_iota(SEGS_EACH, 128)
    lane = last_axis_iota(1, 128)

    def search(i, found):
        return found + jnp.where(page_buf[pl.ds(i, 1), :] == own_pages, lane + i * 128, 0)

    found = lax.fori_loop(0, SEGS_EACH, search, jnp.zeros((SEGS_EACH, 128), jnp.int32))
    segment_col = jnp.sum(found.astype(jnp.float32), axis=1, keepdims=True)
    loader_col = (segment_col.astype(jnp.int32) * INV_SEGS) >> 20
    loader_row = as_row(loader_col.astype(jnp.float32)).astype(jnp.int32)
    is_earlier = as_row(segment_col) < segment_col
    earlier_col = jnp.sum(
        jnp.where(loader_row == loader_col, jnp.where(is_earlier, 1.0, 0.0), 0.0),
        axis=1,
        keepdims=True,
    ).astype(jnp.int32)
    loader_plane = (loader_col >> 5) * 2 + (loader_col & 1)
    loader_z = (loader_col >> 1) & (NZ - 1)
    slot = last_axis_iota(SEGS_EACH, slots)
    slot_by_plane = loader_plane * (NZ * CAP) + loader_z * CAP + earlier_col
    slot_by_z = loader_z * (NQ * CAP) + loader_plane * CAP + earlier_col
    take_by_plane = jnp.where(slot == slot_by_plane, 1.0, 0.0).astype(jnp.bfloat16)
    take_by_z = jnp.where(slot == slot_by_z, 1.0, 0.0).astype(jnp.bfloat16)

    send_z(1, reorder(to_z_order, arrived_p(1)))
    send_p(0, reorder(to_plane_order, arrived_z(0)))
    landed = arrived_p(0)
    first = reorder(take_by_plane, landed)
    out_buf[0] = first[:, :LAT]
    out_copies = [pltpu.make_async_copy(out_buf.at[i], out_hbm.at[i], o_sem.at[i]) for i in range(2)]
    out_copies[0].start()
    out_buf[1, :, RANK:] = first[:, LAT:]

    for rho in range(2):
        for pair in y_copies[rho]:
            for copy in pair:
                copy.wait_send()
        each(NQ, plane, lambda other: p_copy(rho, other).wait_send())
        each_z(lambda other: z_copy(rho, other).wait_send())
    out_buf[1, :, :RANK] = reorder(take_by_z, arrived_z(1))
    out_copies[1].start()
    for copy in out_copies:
        copy.wait()


def shards(hidden_rows, compress_weight, latent_gain, segment_page, segment_length, segment_start):
    half = (LAT - RANK) // 2
    exponent = np.arange(half, dtype=np.float64) * (2.0 / (LAT - RANK))
    frequency = jnp.asarray(np.power(10000.0, -exponent).reshape(1, half).astype(np.float32))
    width = hidden_rows.shape[-1]
    any_spec = pl.BlockSpec(memory_space=pltpu.HBM)
    dma = pltpu.SemaphoreType.DMA
    bf16, f32 = jnp.bfloat16, jnp.float32
    n = SEGS_EACH
    scratch = [
        pltpu.VMEM((TP, 2, n, width), bf16),
        pltpu.VMEM((LAT, width), bf16),
        pltpu.VMEM((1, RANK), f32),
        pltpu.VMEM((n, 128), jnp.int32),
        pltpu.VMEM((n, 128), jnp.int32),
        pltpu.VMEM((n, 128), jnp.int32),
        pltpu.VMEM((1, half), f32),
        pltpu.VMEM((TP - 1, n, WIDE), f32),
        pltpu.VMEM((TP - 1, n, RANK), f32),
        pltpu.VMEM((TP - 1, n, WIDE), jnp.int16),
        pltpu.VMEM((TP - 1, n, RANK), jnp.int16),
        pltpu.VMEM((TP - 1, n, WIDE), jnp.int16),
        pltpu.VMEM((TP - 1, n, RANK), jnp.int16),
        pltpu.VMEM((2, 6, 8, 128), f32),
        pltpu.VMEM((2, 6, 8, 128), f32),
        pltpu.VMEM((NZ, NQ * CAP, WIDE), bf16),
        pltpu.VMEM((NZ, NQ * CAP, RANK), bf16),
        pltpu.VMEM((NZ, NQ * CAP, WIDE), bf16),
        pltpu.VMEM((NZ, NQ * CAP, RANK), bf16),
        pltpu.VMEM((NQ, NZ * CAP, WIDE), bf16),
        pltpu.VMEM((NQ, NZ * CAP, RANK), bf16),
        pltpu.VMEM((NQ, NZ * CAP, WIDE), bf16),
        pltpu.VMEM((NQ, NZ * CAP, RANK), bf16),
        pltpu.VMEM((2, n, LAT), bf16),
        dma((TP,)),
        dma((W_PIECES,)),
        dma((5,)),
        dma((2, 6)),
        dma((2, 6)),
        dma((2, 6)),
        dma((2, 6)),
        dma((2, NZ)),
        dma((2, NZ)),
        dma((2, NQ)),
        dma((2, NQ)),
        dma((2,)),
    ]
    return pl.pallas_call(
        kernel,
        out_shape=jax.ShapeDtypeStruct((2, n, LAT), bf16),
        in_specs=[any_spec] * 7,
        out_specs=any_spec,
        scratch_shapes=scratch,
        compiler_params=pltpu.CompilerParams(
            collective_id=0, has_side_effects=True, vmem_limit_bytes=60 * 1024 * 1024
        ),
        cost_estimate=pl.CostEstimate(
            flops=2 * 8 * n * width * LAT, bytes_accessed=7_000_000, transcendentals=0
        ),
        name="latent_rows",
    )(
        hidden_rows,
        compress_weight.T,
        latent_gain.reshape(1, RANK),
        segment_page.reshape(n, 128),
        segment_length.reshape(n, 128),
        segment_start.reshape(n, 128),
        frequency,
    )


def solution(mesh):
    in_specs = (P(None, "dec", "tp"), P("tp", None), P(), P(), P(), P())
    out_specs = P("tp", "dec", None)
    return jax.shard_map(shards, mesh=mesh, in_specs=in_specs, out_specs=out_specs, check_vma=False)
```
